32 devices in a mesh: section: 4 (over y, core), tensor: 8 (over z, x).
Axes of the slice: x: 2, y: 2, z: 4, core: 2. Of those that a mesh axis runs over, the one named last changes fastest.
Arguments:
- resid: bfloat16 [32, 4608], P('section', 'tensor'), may hold values from -6 to 6
- pre_gain: float32 [4, 4608], P('section'), may hold values from 0.5 to 1.5
- post_gain: float32 [4, 4608], P('section'), may hold values from 0.5 to 1.5
- w_query: bfloat16 [4, 4608, 4096], P('section', None, 'tensor'), may hold values from -0.09375 to 0.09375
- w_key: bfloat16 [4, 4608, 2048], P('section', None, 'tensor'), may hold values from -0.09375 to 0.09375
- w_value: bfloat16 [4, 4608, 2048], P('section', None, 'tensor'), may hold values from -0.09375 to 0.09375
- w_out: bfloat16 [4, 4096, 4608], P('section', 'tensor'), may hold values from -0.09375 to 0.09375
- key_cache: bfloat16 [4, 32, 16, 64, 128], P('section', None, 'tensor'), may hold values from -6 to 6
- value_cache: bfloat16 [4, 32, 16, 64, 128], P('section', None, 'tensor'), may hold values from -6 to 6
- lengths: int32 [32], replicated, may hold values from 1 to 64, as said below
- concept: int32 [32], replicated, may hold values from 0 to 511
- steer_layer: int32 [32], replicated, may hold values from 0 to 3
- strength: float32 [32], replicated, may hold values from 0.5 to 2
- directions: bfloat16 [512, 4608], P(None, 'tensor'), may hold values from -6 to 6
Outputs:
- final_resid: bfloat16 [32, 4608], P('section', 'tensor')
The draws below stay inside these ranges and needn't reach their ends.
Inputs may be any that keep to these rules, and one draw needn't show every extreme that they name: `lengths`: some row of every draw has exactly 64.
All inputs are finite; a program needn't handle non-finite values.
Results may differ from the reference program's by a relative error of at most 0.03.
Values may be sent and summed in bfloat16 or wider, within the bound.
A program may use at most 64 MiB of HBM per device.

```python
import math
import jax
import jax.numpy as jnp
import numpy as np
from jax import lax

D = 4608
HEADS = 32
KVH = 16
HD = 128
CONCEPTS = 512
CTX = 64
ROWS = 32
LAYERS = 4


def draw_lengths(key, part):
    values = jax.random.randint(key, (ROWS,), 1, CTX + 1, dtype=jnp.int32)
    return values.at[0].set(CTX)


def touch_ends(result, stream_key, low, high):
    spot = [jax.random.randint(jax.random.fold_in(stream_key, axis), (), 0, length) for axis, length in enumerate(result.shape)]
    widest = result.shape.index(max(result.shape))
    neighbour = spot[:widest] + [(spot[widest] + 1) % result.shape[widest]] + spot[widest + 1:]
    return result.at[tuple(spot)].set(low).at[tuple(neighbour)].set(high)


def levels(own_key, dims, cuts, smallest, high):
    loudness = 1.0
    for dim, shards_of in cuts:
        heights = jax.random.uniform(jax.random.fold_in(jax.random.fold_in(own_key, 6), dim), (shards_of,), jnp.float32, smallest / len(cuts), high / len(cuts))
        loudness = loudness * jnp.repeat(jnp.exp(heights), dims[dim] // shards_of).reshape((-1,) + (1,) * (len(dims) - 1 - dim))
    return loudness


def rank_table(amount, slope):
    portions = [(1 << 20) // math.isqrt(rank ** slope) + 1 for rank in range(1, amount + 1)]
    deviation = 1 + sum(portions) // (1 << 30)
    return np.cumsum(np.array([max(1, weight // deviation) for weight in portions]))


def skewed_ids(stream_key, shape, count, lean):
    grid = rank_table(count, lean)
    lot = jax.random.randint(jax.random.fold_in(stream_key, 1), shape, 0, int(grid[count - 1]))
    standing = jnp.searchsorted(jnp.asarray(grid, jnp.int32), lot, side="right")
    return jax.random.permutation(jax.random.fold_in(stream_key, 2), count)[standing].astype(jnp.int32)


def scatter_about(rng, shape, scale, bound, pieces=(), kind=jnp.bfloat16):
    entries = scale * jax.random.normal(rng, shape, jnp.float32)
    if pieces:
        entries = entries * levels(rng, shape, pieces, -0.22, 0.18)
    return jnp.clip(entries, -bound, bound).astype(kind)


def setup_inputs(seed: int = 0) -> dict:
    streams_of = jax.random.split(jax.random.key(seed), 15)
    return {
        "resid": scatter_about(streams_of[0], (ROWS, D), 1.0, 6.0, ((0, 4), (1, 8))),
        "pre_gain": jnp.clip(1.0 + 0.1 * jax.random.normal(streams_of[1], (LAYERS, D), jnp.float32), 0.5, 1.5),
        "post_gain": jnp.clip(1.0 + 0.1 * jax.random.normal(streams_of[2], (LAYERS, D), jnp.float32), 0.5, 1.5),
        "w_query": scatter_about(streams_of[3], (LAYERS, D, HEADS * HD), D ** -0.5, 0.09375, ((0, 4), (2, 8))),
        "w_key": scatter_about(streams_of[4], (LAYERS, D, KVH * HD), D ** -0.5, 0.09375, ((0, 4), (2, 8))),
        "w_value": scatter_about(streams_of[5], (LAYERS, D, KVH * HD), D ** -0.5, 0.09375, ((0, 4), (2, 8))),
        "w_out": scatter_about(streams_of[6], (LAYERS, HEADS * HD, D), (HEADS * HD) ** -0.5, 0.09375, ((0, 4), (1, 8))),
        "key_cache": scatter_about(streams_of[7], (LAYERS, ROWS, KVH, CTX, HD), 1.0, 6.0, ((0, 4), (2, 8))),
        "value_cache": scatter_about(streams_of[8], (LAYERS, ROWS, KVH, CTX, HD), 1.0, 6.0, ((0, 4), (2, 8))),
        "lengths": draw_lengths(jax.random.fold_in(streams_of[14], 71), 0),
        "concept": touch_ends(skewed_ids(streams_of[10], (ROWS,), CONCEPTS, 2), jax.random.fold_in(streams_of[10], 3), 0, CONCEPTS - 1).astype(jnp.int32),
        "steer_layer": touch_ends(jax.random.randint(streams_of[11], (ROWS,), 0, LAYERS), jax.random.fold_in(streams_of[11], 1), 0, LAYERS - 1).astype(jnp.int32),
        "strength": jnp.clip(jax.random.uniform(streams_of[12], (ROWS,), jnp.float32, 0.5, 2.0), 0.5, 2.0),
        "directions": scatter_about(streams_of[13], (CONCEPTS, D), 1.0, 6.0, ((1, 8),)),
    }


epsilon = 1e-06
softcap_limit = 50.0

def rotate(vectors, places):
    half_dim = vectors.shape[-1] // 2
    frequency = 10000.0 ** (-(jnp.arange(half_dim, dtype=jnp.float32) * 2.0) / vectors.shape[-1])
    angles = places[:, None, None] * frequency[None, None, :]
    first = vectors[..., :half_dim]
    second = vectors[..., half_dim:]
    cosine = jnp.cos(angles)
    sine = jnp.sin(angles)
    return jnp.concatenate([first * cosine - second * sine, second * cosine + first * sine], axis=-1)

def attend(queries, new_keys, new_values, cache_keys, cache_values, row_lengths, scale):
    scores = jnp.einsum('rkgd,rkcd->rkgc', queries.astype(jnp.float32), cache_keys.astype(jnp.float32)) * scale
    own_score = jnp.einsum('rkgd,rkd->rkg', queries.astype(jnp.float32), new_keys.astype(jnp.float32)) * scale
    capped = softcap_limit * jnp.tanh(scores / softcap_limit)
    own_capped = softcap_limit * jnp.tanh(own_score / softcap_limit)
    valid = jnp.arange(cache_keys.shape[2], dtype=jnp.int32)[None, :] < row_lengths[:, None]
    weights = jnp.where(valid[:, None, None, :], jnp.exp(capped - softcap_limit), jnp.float32(0.0))
    own_weight = jnp.exp(own_capped - softcap_limit)
    totals = lax.optimization_barrier(jnp.sum(weights, axis=-1)) + own_weight
    probs = (weights / totals[..., None]).astype(jnp.bfloat16)
    own_prob = (own_weight / totals).astype(jnp.bfloat16)
    mixed = jnp.einsum('rkgc,rkcd->rkgd', probs.astype(jnp.float32), cache_values.astype(jnp.float32))
    return mixed + own_prob.astype(jnp.float32)[..., None] * new_values.astype(jnp.float32)[:, :, None, :]

def reference(resid, pre_gain, post_gain, w_query, w_key, w_value, w_out, key_cache, value_cache, lengths, concept, steer_layer, strength, directions):
    group = HEADS // KVH
    scale = float(D // HEADS) ** (-0.5)
    places = lengths.astype(jnp.float32)
    steer_vectors = directions[concept].astype(jnp.float32)
    current = resid
    for layer_index in range(LAYERS):
        values_full = current.astype(jnp.float32)
        normed = (values_full * lax.rsqrt(lax.optimization_barrier(jnp.mean(values_full * values_full, axis=-1, keepdims=True)) + epsilon) * pre_gain[layer_index]).astype(jnp.bfloat16)
        queries = rotate(jnp.dot(normed, w_query[layer_index], preferred_element_type=jnp.float32).reshape(ROWS, HEADS, HD), places).astype(jnp.bfloat16)
        new_keys = rotate(jnp.dot(normed, w_key[layer_index], preferred_element_type=jnp.float32).reshape(ROWS, KVH, HD), places).astype(jnp.bfloat16)
        new_values = jnp.dot(normed, w_value[layer_index], preferred_element_type=jnp.float32).astype(jnp.bfloat16).reshape(ROWS, KVH, HD)
        mixed = attend(queries.reshape(ROWS, KVH, group, HD), new_keys, new_values, key_cache[layer_index], value_cache[layer_index], lengths, scale)
        heads_out = mixed.reshape(ROWS, HEADS * HD).astype(jnp.bfloat16)
        summed = jnp.dot(heads_out, w_out[layer_index], preferred_element_type=jnp.float32)
        post = summed * lax.rsqrt(lax.optimization_barrier(jnp.mean(summed * summed, axis=-1, keepdims=True)) + epsilon) * post_gain[layer_index]
        steer_gate = strength * (steer_layer == layer_index).astype(jnp.float32)
        current = (values_full + post + steer_gate[:, None] * steer_vectors).astype(jnp.bfloat16)
    return current
```

```python
import functools
import math

import jax
import jax.numpy as jnp
from jax import lax
from jax.experimental import pallas as pl
from jax.experimental.pallas import tpu as pltpu
from jax.sharding import PartitionSpec as P

MESH = pl.DeviceIdType.MESH
epsilon = 1e-06
softcap_limit = 50.0
BLOCK = 16
f32 = jnp.float32
bf16 = jnp.bfloat16


def kernel(
    S, T,
    lengths, concept, steer_layer, strength,
    resid, pre, post, wq, wk, wv, wo, kc, vc, dirs,
    out_ref,
    wq_v, wk_v, wv_v, wo_v, kc_v, vc_v, dirs_v,
    xg, xprev, x_ref, base, st, dself, gates, lens,
    qs, ks, vs, heads, part, rs, msg, ag, fin_x, fin_p, fin_s, fin_f,
    w_sem, xg_ss, xg_rs, xf_sem, st_ss, st_rs, rs_ss, rs_rs, ag_ss, ag_rs,
    fx_ss, fx_rs, fp_ss, fp_rs, fs_ss, fs_rs,
):
    s = lax.axis_index("section")
    t = lax.axis_index("tensor")
    N = S * T
    R, D = x_ref.shape
    rc, W = resid.shape
    HD = kc_v.shape[-1]
    CTX = kc_v.shape[2]
    KL = kc_v.shape[1]
    H = qs.shape[0]
    group = H // KL
    G = R // BLOCK
    F = T // G
    C = D // F
    per = T // F
    sper = BLOCK // rc
    last = S - 1
    half = HD // 2
    scale = float(D // (H * T)) ** (-0.5)

    def wait(ref, sem):
        pltpu.make_async_copy(ref, ref, sem).wait()

    def remote(src, dst, ss, rsem, ds, dt):
        return pltpu.make_async_remote_copy(
            src_ref=src, dst_ref=dst, send_sem=ss, recv_sem=rsem,
            device_id=(ds, dt), device_id_type=MESH)

    def send(src, dst, ss, rsem, ds, dt):
        mine = (ds == s) & (dt == t)

        @pl.when(mine)
        def _():
            pltpu.make_async_copy(src, dst, rsem).start()

        @pl.when(jnp.logical_not(mine))
        def _():
            remote(src, dst, ss, rsem, ds, dt).start()

    def sent(src, ss, ds, dt):
        @pl.when(jnp.logical_not((ds == s) & (dt == t)))
        def _():
            wait(src, ss)

    loads = [
        pltpu.make_async_copy(a.at[0], b, w_sem.at[i])
        for i, (a, b) in enumerate(
            [(wq, wq_v), (wk, wk_v), (wv, wv_v), (kc, kc_v), (vc, vc_v), (wo, wo_v)])
    ] + [pltpu.make_async_copy(dirs, dirs_v, w_sem.at[6])]
    for one in loads:
        one.start()

    barrier = pltpu.get_barrier_semaphore()
    me = s * T + t

    def greet(n, carry):
        other = lax.rem(me + n, N)
        pl.semaphore_signal(barrier, inc=1, device_id=(other // T, lax.rem(other, T)),
                            device_id_type=MESH)
        return carry

    lax.fori_loop(1, N, greet, 0)
    pl.semaphore_wait(barrier, N - 1)

    for k in range(T):
        dt = lax.rem(t + k, T)
        send(resid, xg.at[s, t], xg_ss.at[k], xg_rs.at[s, t], 0, dt)

    rows = lax.broadcasted_iota(jnp.int32, (R, HD), 0)
    zero_i = jnp.zeros((R, HD), jnp.int32)

    def gather(i, carry):
        a, b, c, d = carry
        hit = rows == i
        return (jnp.where(hit, lengths[i], a), jnp.where(hit, concept[i], b),
                jnp.where(hit, steer_layer[i], c), jnp.where(hit, strength[i], d))

    len_v, con_v, lay_v, str_v = lax.fori_loop(
        0, R, gather, (zero_i, zero_i, zero_i, jnp.zeros((R, HD), f32)))
    lens[...] = len_v
    gates[...] = str_v * (lay_v == last).astype(f32)
    lane = lax.broadcasted_iota(jnp.int32, (R, HD), 1)
    frequency = jnp.exp(lax.rem(lane, half).astype(f32) * (-2.0 * math.log(10000.0) / HD))
    angle = len_v.astype(f32) * frequency
    cosine = jnp.cos(angle)
    sine = jnp.sin(angle)
    sine = jnp.where(lane < half, -sine, sine)

    loads[6].wait()
    nc = dirs_v.shape[0]
    one_hot = (con_v[:, 0:1] == lax.broadcasted_iota(jnp.int32, (R, nc), 1)).astype(f32).astype(bf16)
    picked = jnp.dot(one_hot, dirs_v[...], preferred_element_type=f32)
    dself[...] = picked

    @pl.when(s == 0)
    def _():
        for a in range(S):
            for b in range(T):
                wait(xg.at[a, b], xg_rs.at[a, b])
            base[a * rc:(a + 1) * rc, :] = jnp.concatenate(
                [xg[a, b].astype(f32) for b in range(T)], axis=1)

    @pl.when(s > 0)
    def _():
        st[t] = picked.astype(bf16)
        wait(xprev, xf_sem.at[1])
        for k in range(1, T):
            dt = lax.rem(t + k, T)
            remote(st.at[t], st.at[t], st_ss.at[k], st_rs.at[t], s, dt).start()
        for k in range(1, T):
            b = lax.rem(t + k, T)
            wait(st.at[b], st_rs.at[b])
        gate = (str_v * (lay_v == s - 1).astype(f32))[:, 0:1]
        full = jnp.concatenate([st[b].astype(f32) for b in range(T)], axis=1)
        base[...] = xprev[...].astype(f32) + gate * full
        for o in range(T):
            wait(ag.at[o], ag_rs.at[o])
        for rg in range(G):
            total = jnp.zeros((BLOCK, 1), f32)
            for q in range(F):
                tail = ag[rg * F + q, :, C:C + 128].astype(f32)
                total = total + tail[:, 0:1] + tail[:, 64:65]
            inv = lax.rsqrt(total / D + epsilon)
            for q in range(F):
                place = (slice(rg * BLOCK, (rg + 1) * BLOCK), slice(q * C, (q + 1) * C))
                base[place] = base[place] + inv * ag[rg * F + q, :, 0:C].astype(f32)

    x_bf = base[...].astype(bf16)
    x_ref[...] = x_bf

    my_rg = t // F
    my_q = lax.rem(t, F)
    my_cols = pl.ds(pl.multiple_of(my_q * C, 128), C)
    x_piece = x_ref.at[pl.ds(pl.multiple_of(my_rg * BLOCK, BLOCK), BLOCK), my_cols]
    takers = [(my_rg * sper + a, my_q * per + b, a * per + b)
              for a in range(sper) for b in range(per)]

    @pl.when(s < last)
    def _():
        remote(x_ref, xprev, xf_sem.at[0], xf_sem.at[1], s + 1, t).start()

    @pl.when(s == last)
    def _():
        for ds, dt, n in takers:
            send(x_piece, fin_x, fx_ss.at[n], fx_rs, ds, dt)

    xf = x_bf.astype(f32)
    inv = lax.rsqrt(jnp.mean(xf * xf, axis=1, keepdims=True) + epsilon)
    normed = (xf * inv * pre[...]).astype(bf16)

    def rope(v):
        return (v * cosine + pltpu.roll(v, half, 1) * sine).astype(bf16).astype(f32)

    loads[0].wait()
    q_all = jnp.dot(normed, wq_v[...], preferred_element_type=f32)
    for h in range(H):
        qs[h] = rope(q_all[:, h * HD:(h + 1) * HD])
    loads[1].wait()
    k_all = jnp.dot(normed, wk_v[...], preferred_element_type=f32)
    loads[2].wait()
    v_all = jnp.dot(normed, wv_v[...], preferred_element_type=f32)
    for h in range(KL):
        ks[h] = rope(k_all[:, h * HD:(h + 1) * HD])
        vs[h] = v_all[:, h * HD:(h + 1) * HD].astype(bf16).astype(f32)

    loads[3].wait()
    loads[4].wait()
    span = 8 * CTX
    col = lax.broadcasted_iota(jnp.int32, (8 * group, span), 1)
    row = lax.broadcasted_iota(jnp.int32, (8 * group, span), 0)
    same = (col // CTX) == lax.rem(row, 8)
    spot = lax.rem(col, CTX)
    for i in range(R // 8):
        r0 = 8 * i
        limit = jnp.concatenate([lens[r0:r0 + 8, 0:1]] * group, axis=0)
        valid = same & (spot < limit)
        for h in range(KL):
            qq = jnp.concatenate([qs[h * group + g, r0:r0 + 8, :] for g in range(group)], axis=0)
            kk = jnp.concatenate([ks[h, r0:r0 + 8, :]] * group, axis=0)
            vv = jnp.concatenate([vs[h, r0:r0 + 8, :]] * group, axis=0)
            keys = kc_v[r0:r0 + 8, h].reshape(span, HD)
            values = vc_v[r0:r0 + 8, h].reshape(span, HD)
            scores = lax.dot_general(qq.astype(bf16), keys, (((1,), (1,)), ((), ())),
                                     preferred_element_type=f32) * scale
            own = jnp.sum(qq * kk, axis=1, keepdims=True) * scale
            weight = jnp.where(
                valid,
                jnp.exp(softcap_limit * jnp.tanh(scores / softcap_limit) - softcap_limit), 0.0)
            own_w = jnp.exp(softcap_limit * jnp.tanh(own / softcap_limit) - softcap_limit)
            total = jnp.sum(weight, axis=1, keepdims=True) + own_w
            probs = (weight / total).astype(bf16)
            own_p = (own_w / total).astype(bf16).astype(f32)
            mixed = jnp.dot(probs, values, preferred_element_type=f32) + own_p * vv
            for g in range(group):
                c0 = (h * group + g) * HD
                heads[r0:r0 + 8, c0:c0 + HD] = mixed[8 * g:8 * g + 8, :]

    heads_bf = heads[...].astype(bf16)
    loads[5].wait()
    for q in range(F):
        res = jnp.dot(heads_bf, wo_v[:, q * C:(q + 1) * C],
                      preferred_element_type=f32).astype(bf16)
        for rg in range(G):
            o = rg * F + q
            part[o] = res[rg * BLOCK:(rg + 1) * BLOCK, :]
            send(part.at[o], rs.at[t], rs_ss.at[o], rs_rs.at[t], s, o)

    summed = jnp.zeros((BLOCK, C), f32)
    for o in range(T):
        wait(rs.at[o], rs_rs.at[o])
        summed = summed + rs[o].astype(f32)
    squares = jnp.sum(summed * summed, axis=1, keepdims=True)
    high = squares.astype(bf16).astype(f32)
    msg[:, 0:C] = (summed * post[:, my_cols]).astype(bf16)
    tail_lane = lax.broadcasted_iota(jnp.int32, (BLOCK, 128), 1)
    msg[:, C:C + 128] = jnp.where(tail_lane < 64, high, squares - high).astype(bf16)

    @pl.when(s < last)
    def _():
        for k in range(T):
            dt = lax.rem(t + k, T)
            remote(msg, ag.at[t], ag_ss.at[k], ag_rs.at[t], s + 1, dt).start()

    @pl.when(s == last)
    def _():
        for ds, dt, n in takers:
            send(msg.at[:, pl.ds(0, C)], fin_p, fp_ss.at[n], fp_rs, ds, dt)
        for a in range(sper):
            for b in range(T):
                send(msg.at[:, pl.ds(C, 128)], fin_s.at[my_q], fs_ss.at[a * T + b],
                     fs_rs.at[my_q], my_rg * sper + a, b)

    wait(fin_x, fx_rs)
    wait(fin_p, fp_rs)
    total = jnp.zeros((BLOCK, 1), f32)
    for q in range(F):
        wait(fin_s.at[q], fs_rs.at[q])
        tail = fin_s[q].astype(f32)
        total = total + tail[:, 0:1] + tail[:, 64:65]
    inv = lax.rsqrt(total / D + epsilon)
    fin_f[...] = fin_x[...].astype(f32) + inv * fin_p[...].astype(f32)
    here = fin_f[pl.ds(pl.multiple_of(lax.rem(s, sper) * rc, rc), rc), :]
    within = lax.rem(t, per)
    piece = here[:, 0:W]
    for b in range(1, per):
        piece = jnp.where(within == b, here[:, b * W:(b + 1) * W], piece)
    own_rows = pl.ds(pl.multiple_of(s * rc, rc), rc)
    out_ref[...] = (piece + gates[own_rows, :][:, 0:1] * dself[own_rows, :]).astype(bf16)

    for k in range(T):
        sent(resid, xg_ss.at[k], 0, lax.rem(t + k, T))
    for o in range(T):
        sent(part.at[o], rs_ss.at[o], s, o)

    @pl.when(s > 0)
    def _():
        for k in range(1, T):
            wait(st.at[t], st_ss.at[k])

    @pl.when(s < last)
    def _():
        wait(x_ref, xf_sem.at[0])
        for k in range(T):
            wait(msg, ag_ss.at[k])

    @pl.when(s == last)
    def _():
        for ds, dt, n in takers:
            sent(x_piece, fx_ss.at[n], ds, dt)
            sent(msg.at[:, pl.ds(0, C)], fp_ss.at[n], ds, dt)
        for a in range(sper):
            for b in range(T):
                sent(msg.at[:, pl.ds(C, 128)], fs_ss.at[a * T + b], my_rg * sper + a, b)


def on_device(
    S, T,
    resid, pre_gain, post_gain, w_query, w_key, w_value, w_out, key_cache, value_cache,
    lengths, concept, steer_layer, strength, directions,
):
    rc, W = resid.shape
    R = lengths.shape[0]
    D = pre_gain.shape[1]
    HD = key_cache.shape[-1]
    H = w_query.shape[2] // HD
    KL = key_cache.shape[2]
    G = R // BLOCK
    F = T // G
    C = D // F
    per = T // F
    sper = BLOCK // rc
    dma = pltpu.SemaphoreType.DMA
    vm = pltpu.VMEM
    smem = pl.BlockSpec(memory_space=pltpu.SMEM)
    vmem = pl.BlockSpec(memory_space=pltpu.VMEM)
    hbm = pl.BlockSpec(memory_space=pl.ANY)
    scratch = [
        vm(w_query.shape[1:], bf16), vm(w_key.shape[1:], bf16), vm(w_value.shape[1:], bf16),
        vm(w_out.shape[1:], bf16), vm(key_cache.shape[1:], bf16), vm(value_cache.shape[1:], bf16),
        vm(directions.shape, bf16),
        vm((S, T, rc, W), bf16), vm((R, D), bf16), vm((R, D), bf16), vm((R, D), f32),
        vm((T, R, W), bf16), vm((R, W), f32), vm((R, HD), f32), vm((R, HD), jnp.int32),
        vm((H, R, HD), f32), vm((KL, R, HD), f32), vm((KL, R, HD), f32), vm((R, H * HD), f32),
        vm((T, BLOCK, C), bf16), vm((T, BLOCK, C), bf16), vm((BLOCK, C + 128), bf16),
        vm((T, BLOCK, C + 128), bf16), vm((BLOCK, C), bf16), vm((BLOCK, C), bf16),
        vm((F, BLOCK, 128), bf16), vm((BLOCK, C), f32),
        dma((7,)), dma((T,)), dma((S, T)), dma((2,)), dma((T,)), dma((T,)), dma((T,)), dma((T,)),
        dma((T,)), dma((T,)),
        dma((sper * per,)), dma, dma((sper * per,)), dma, dma((sper * T,)), dma((F,)),
    ]
    return pl.pallas_call(
        functools.partial(kernel, S, T),
        out_shape=jax.ShapeDtypeStruct((rc, W), bf16),
        in_specs=[smem] * 4 + [vmem] * 3 + [hbm] * 7,
        out_specs=vmem,
        scratch_shapes=scratch,
        compiler_params=pltpu.CompilerParams(
            collective_id=0, has_side_effects=True, vmem_limit_bytes=48 * 1024 * 1024),
    )(lengths, concept, steer_layer, strength, resid, pre_gain, post_gain,
      w_query, w_key, w_value, w_out, key_cache, value_cache, directions)


def solution(mesh):
    placed = (
        P("section", "tensor"),
        P("section", None),
        P("section", None),
        P("section", None, "tensor"),
        P("section", None, "tensor"),
        P("section", None, "tensor"),
        P("section", "tensor", None),
        P("section", None, "tensor", None, None),
        P("section", None, "tensor", None, None),
        P(),
        P(),
        P(),
        P(),
        P(None, "tensor"),
    )
    S, T = mesh.shape["section"], mesh.shape["tensor"]
    return jax.shard_map(
        functools.partial(on_device, S, T), mesh=mesh, in_specs=placed,
        out_specs=P("section", "tensor"), check_vma=False,
    )
```

```python
import functools
import math

import jax
import jax.numpy as jnp
from jax import lax
from jax.experimental import pallas as pl
from jax.experimental.pallas import tpu as pltpu
from jax.sharding import PartitionSpec as P

MESH = pl.DeviceIdType.MESH
epsilon = 1e-06
softcap_limit = 50.0
BLOCK = 16
f32 = jnp.float32
bf16 = jnp.bfloat16


def kernel(
    S, T,
    lengths_h, concept_h, steer_h, strength_h,
    resid_h, pre_h, post_h, wq, wk, wv, wo, kc, vc, dirs,
    out_ref,
    lengths, concept, steer_layer, strength, resid, pre, post,
    wq_v, wk_v, wv_v, wo_v, kc_v, vc_v, dirs_v,
    xg, xprev, x_ref, base, st, dself, gates, lens,
    qs, ks, vs, heads, part, rs, msg, ag, fin_x, fin_p, fin_s, fin_f,
    w_sem, xg_ss, xg_rs, xf_ss, xf_rs, st_ss, st_rs, rs_ss, rs_rs, ag_ss, ag_rs,
    fx_ss, fx_rs, fp_ss, fp_rs, fs_ss, fs_rs,
):
    s = lax.axis_index("section")
    t = lax.axis_index("tensor")
    N = S * T
    G, _, D = x_ref.shape
    R = G * BLOCK
    rc, W = resid.shape
    HD = kc_v.shape[-1]
    CTX = kc_v.shape[2]
    KL = kc_v.shape[1]
    H = qs.shape[0]
    group = H // KL
    chunks = D // 128
    Wp = fin_f.shape[1]
    sper = BLOCK // rc
    last = S - 1
    half = HD // 2
    scale = float(D // (H * T)) ** (-0.5)

    def begin(o):
        return (o * chunks) // T * 128

    def window(o):
        return pl.ds(pl.multiple_of(begin(o), 128), Wp)

    def wait(ref, sem):
        pltpu.make_async_copy(ref, ref, sem).wait()

    def remote(src, dst, ss, rsem, ds, dt):
        return pltpu.make_async_remote_copy(
            src_ref=src, dst_ref=dst, send_sem=ss, recv_sem=rsem,
            device_id=(ds, dt), device_id_type=MESH)

    def send(src, dst, ss, rsem, ds, dt):
        mine = (ds == s) & (dt == t)

        @pl.when(mine)
        def _():
            pltpu.make_async_copy(src, dst, rsem).start()

        @pl.when(jnp.logical_not(mine))
        def _():
            remote(src, dst, ss, rsem, ds, dt).start()

    def sent(src, ss, ds, dt):
        @pl.when(jnp.logical_not((ds == s) & (dt == t)))
        def _():
            wait(src, ss)

    barrier = pltpu.get_barrier_semaphore()
    me = s * T + t

    def greet(n, carry):
        other = lax.rem(me + n, N)
        pl.semaphore_signal(barrier, inc=1, device_id=(other // T, lax.rem(other, T)),
                            device_id_type=MESH)
        return carry

    lax.fori_loop(1, N, greet, 0)

    pairs = [(resid_h, resid), (lengths_h, lengths), (concept_h, concept), (steer_h, steer_layer),
             (strength_h, strength), (pre_h, pre), (post_h, post), (dirs, dirs_v),
             (wq.at[0], wq_v), (wk.at[0], wk_v), (wv.at[0], wv_v), (kc.at[0], kc_v),
             (vc.at[0], vc_v), (wo.at[0], wo_v)]
    loads = [pltpu.make_async_copy(a, b, w_sem.at[i]) for i, (a, b) in enumerate(pairs)]
    for one in loads:
        one.start()
    loads[0].wait()
    pl.semaphore_wait(barrier, N - 1)

    for k in range(T):
        dt = lax.rem(t + k, T)
        send(resid, xg.at[s, t], xg_ss.at[k], xg_rs.at[s, t], 0, dt)

    for n in range(1, 7):
        loads[n].wait()
    rows = lax.broadcasted_iota(jnp.int32, (R, HD), 0)
    zero_i = jnp.zeros((R, HD), jnp.int32)

    def gather(i, carry):
        a, b, c, d = carry
        hit = rows == i
        return (jnp.where(hit, lengths[i], a), jnp.where(hit, concept[i], b),
                jnp.where(hit, steer_layer[i], c), jnp.where(hit, strength[i], d))

    len_v, con_v, lay_v, str_v = lax.fori_loop(
        0, R, gather, (zero_i, zero_i, zero_i, jnp.zeros((R, HD), f32)))
    lens[...] = len_v
    gates[...] = str_v * (lay_v == last).astype(f32)
    lane = lax.broadcasted_iota(jnp.int32, (R, HD), 1)
    frequency = jnp.exp(lax.rem(lane, half).astype(f32) * (-2.0 * math.log(10000.0) / HD))
    angle = len_v.astype(f32) * frequency
    cosine = jnp.cos(angle)
    sine = jnp.sin(angle)
    sine = jnp.where(lane < half, -sine, sine)

    loads[7].wait()
    nc = dirs_v.shape[1]
    one_hot = (con_v[:, 0:1] == lax.broadcasted_iota(jnp.int32, (R, nc), 1)).astype(f32).astype(bf16)
    picked = lax.dot_general(one_hot, dirs_v[...], (((1,), (1,)), ((), ())),
                             preferred_element_type=f32)
    dself[...] = picked

    @pl.when(s > 0)
    def _():
        st[t] = picked.astype(bf16)
        for a in range(G):
            wait(xprev.at[a], xf_rs.at[a])
        for k in range(1, T):
            dt = lax.rem(t + k, T)
            remote(st.at[t], st.at[t], st_ss.at[k], st_rs.at[t], s, dt).start()
        for k in range(1, T):
            b = lax.rem(t + k, T)
            wait(st.at[b], st_rs.at[b])
        gate = (str_v * (lay_v == s - 1).astype(f32))[:, 0:1]
        full = jnp.concatenate([st[b].astype(f32) for b in range(T)], axis=1)
        for a in range(G):
            cut = slice(a * BLOCK, (a + 1) * BLOCK)
            base[a] = xprev[a].astype(f32) + gate[cut] * full[cut]

    my_cols = window(t)
    span = 8 * CTX
    tiles = BLOCK // 8
    height = tiles * KL * 8 * group
    col = lax.broadcasted_iota(jnp.int32, (height, span), 1)
    row = lax.broadcasted_iota(jnp.int32, (height, span), 0)
    same = (col // CTX) == lax.rem(row, 8)
    spot = lax.rem(col, CTX)
    tail_lane = lax.broadcasted_iota(jnp.int32, (BLOCK, 128), 1)
    piece_lane = lax.broadcasted_iota(jnp.int32, (BLOCK, Wp), 1)
    fresh = piece_lane < begin(t + 1) - begin(t)

    def rope(v, cut):
        return (v * cosine[cut] + pltpu.roll(v, half, 1) * sine[cut]).astype(bf16).astype(f32)

    def total_of(ref, index):
        total = jnp.zeros((BLOCK, 1), f32)
        for o in range(T):
            tail = index(ref, o).astype(f32)
            total = total + tail[:, 0:1] + tail[:, 64:65]
        return lax.rsqrt(total / D + epsilon)

    def enter(a):
        @pl.when(s == 0)
        def _():
            for n in range(sper):
                owner = a * sper + n
                for b in range(T):
                    wait(xg.at[owner, b], xg_rs.at[owner, b])
                base[a, n * rc:(n + 1) * rc, :] = jnp.concatenate(
                    [xg[owner, b].astype(f32) for b in range(T)], axis=1)

        @pl.when(s > 0)
        def _():
            for o in range(T):
                wait(ag.at[a, o], ag_rs.at[a, o])
            inv = total_of(ag, lambda ref, o: ref[a, o, :, Wp:Wp + 128])
            for o in range(T):
                lo = begin(o)
                size = begin(o + 1) - lo
                base[a, :, lo:lo + size] = (
                    base[a, :, lo:lo + size] + inv * ag[a, o, :, 0:size].astype(f32))

        x_bf = base[a].astype(bf16)
        x_ref[a] = x_bf

        @pl.when(s < last)
        def _():
            remote(x_ref.at[a], xprev.at[a], xf_ss.at[a], xf_rs.at[a], s + 1, t).start()

        @pl.when(s == last)
        def _():
            for n in range(sper):
                send(x_ref.at[a, :, my_cols], fin_x, fx_ss.at[a, n], fx_rs, a * sper + n, t)

        xf = x_bf.astype(f32)
        inv = lax.rsqrt(jnp.mean(xf * xf, axis=1, keepdims=True) + epsilon)
        return (xf * inv * pre[...]).astype(bf16)

    def project(a, normed):
        cut = slice(a * BLOCK, (a + 1) * BLOCK)
        if a == 0:
            loads[8].wait()
        q_all = jnp.dot(normed, wq_v[...], preferred_element_type=f32)
        for h in range(H):
            qs[h] = rope(q_all[:, h * HD:(h + 1) * HD], cut)
        if a == 0:
            loads[9].wait()
            loads[10].wait()
        k_all = jnp.dot(normed, wk_v[...], preferred_element_type=f32)
        v_all = jnp.dot(normed, wv_v[...], preferred_element_type=f32)
        for h in range(KL):
            ks[h] = rope(k_all[:, h * HD:(h + 1) * HD], cut)
            vs[h] = v_all[:, h * HD:(h + 1) * HD].astype(bf16).astype(f32)

    def attend(a):
        if a == 0:
            loads[11].wait()
            loads[12].wait()
        units = [(i, h) for i in range(tiles) for h in range(KL)]
        qq = jnp.concatenate([qs[h * group + g, 8 * i:8 * i + 8, :]
                              for i, h in units for g in range(group)], axis=0)
        kk = jnp.concatenate([ks[h, 8 * i:8 * i + 8, :]
                              for i, h in units for g in range(group)], axis=0)
        vv = jnp.concatenate([vs[h, 8 * i:8 * i + 8, :]
                              for i, h in units for g in range(group)], axis=0)
        r0 = a * BLOCK
        limit = jnp.concatenate([lens[r0 + 8 * i:r0 + 8 * i + 8, 0:1]
                                 for i, h in units for g in range(group)], axis=0)
        qb = qq.astype(bf16)
        step = 8 * group
        scores = jnp.concatenate([
            lax.dot_general(qb[n * step:(n + 1) * step],
                            kc_v[r0 + 8 * i:r0 + 8 * i + 8, h].reshape(span, HD),
                            (((1,), (1,)), ((), ())), preferred_element_type=f32)
            for n, (i, h) in enumerate(units)], axis=0) * scale
        own = jnp.sum(qq * kk, axis=1, keepdims=True) * scale
        weight = jnp.where(
            same & (spot < limit),
            jnp.exp(softcap_limit * jnp.tanh(scores / softcap_limit) - softcap_limit), 0.0)
        own_w = jnp.exp(softcap_limit * jnp.tanh(own / softcap_limit) - softcap_limit)
        total = jnp.sum(weight, axis=1, keepdims=True) + own_w
        probs = (weight / total).astype(bf16)
        own_p = (own_w / total).astype(bf16).astype(f32)
        mixed = jnp.concatenate([
            jnp.dot(probs[n * step:(n + 1) * step],
                    vc_v[r0 + 8 * i:r0 + 8 * i + 8, h].reshape(span, HD),
                    preferred_element_type=f32)
            for n, (i, h) in enumerate(units)], axis=0) + own_p * vv
        for n, (i, h) in enumerate(units):
            for g in range(group):
                c0 = (h * group + g) * HD
                heads[8 * i:8 * i + 8, c0:c0 + HD] = mixed[n * step + 8 * g:n * step + 8 * g + 8, :]

    def leave(a):
        if a == 0:
            loads[13].wait()
        part[a] = jnp.dot(heads[...].astype(bf16), wo_v[...],
                          preferred_element_type=f32).astype(bf16)
        for k in range(1, T):
            dt = lax.rem(t + k, T)
            remote(part.at[a, :, window(dt)], rs.at[a, t], rs_ss.at[a, k], rs_rs.at[a, t],
                   s, dt).start()
        rs[a, t] = part[a, :, my_cols]

    def reduce(a):
        for k in range(1, T):
            o = lax.rem(t + k, T)
            wait(rs.at[a, o], rs_rs.at[a, o])
        summed = jnp.zeros((BLOCK, Wp), f32)
        for o in range(T):
            summed = summed + rs[a, o].astype(f32)
        squares = jnp.sum(jnp.where(fresh, summed * summed, 0.0), axis=1, keepdims=True)
        high = squares.astype(bf16).astype(f32)
        msg[a, :, 0:Wp] = (summed * post[:, my_cols]).astype(bf16)
        msg[a, :, Wp:Wp + 128] = jnp.where(tail_lane < 64, high, squares - high).astype(bf16)

        @pl.when(s < last)
        def _():
            for k in range(T):
                dt = lax.rem(t + k, T)
                remote(msg.at[a], ag.at[a, t], ag_ss.at[a, k], ag_rs.at[a, t], s + 1, dt).start()

        @pl.when(s == last)
        def _():
            for n in range(sper):
                ds = a * sper + n
                send(msg.at[a, :, pl.ds(0, Wp)], fin_p, fp_ss.at[a, n], fp_rs, ds, t)
                for b in range(T):
                    send(msg.at[a, :, pl.ds(Wp, 128)], fin_s.at[t], fs_ss.at[a, n * T + b],
                         fs_rs.at[t], ds, b)

    for a in range(G):
        project(a, enter(a))
        if a > 0:
            reduce(a - 1)
        attend(a)
        leave(a)
    reduce(G - 1)

    wait(fin_x, fx_rs)
    wait(fin_p, fp_rs)
    for o in range(T):
        wait(fin_s.at[o], fs_rs.at[o])
    inv = total_of(fin_s, lambda ref, o: ref[o])
    fin_f[...] = fin_x[...].astype(f32) + inv * fin_p[...].astype(f32)
    here = fin_f[pl.ds(pl.multiple_of(lax.rem(s, sper) * rc, rc), rc), :]
    shift = t * W - begin(t)
    piece = here[:, 0:W]
    for b in sorted({(p * W) % 128 for p in range(T)} - {0}):
        piece = jnp.where(shift == b, here[:, b:b + W], piece)
    own_rows = pl.ds(pl.multiple_of(s * rc, rc), rc)
    out_ref[...] = (piece + gates[own_rows, :][:, 0:1] * dself[own_rows, :]).astype(bf16)

    for k in range(T):
        sent(resid, xg_ss.at[k], 0, lax.rem(t + k, T))
    for a in range(G):
        for k in range(1, T):
            wait(part.at[a, :, window(lax.rem(t + k, T))], rs_ss.at[a, k])

    @pl.when(s > 0)
    def _():
        for k in range(1, T):
            wait(st.at[t], st_ss.at[k])

    @pl.when(s < last)
    def _():
        for a in range(G):
            wait(x_ref.at[a], xf_ss.at[a])
            for k in range(T):
                wait(msg.at[a], ag_ss.at[a, k])

    @pl.when(s == last)
    def _():
        for a in range(G):
            for n in range(sper):
                ds = a * sper + n
                sent(x_ref.at[a, :, my_cols], fx_ss.at[a, n], ds, t)
                sent(msg.at[a, :, pl.ds(0, Wp)], fp_ss.at[a, n], ds, t)
                for b in range(T):
                    sent(msg.at[a, :, pl.ds(Wp, 128)], fs_ss.at[a, n * T + b], ds, b)


def on_device(
    S, T,
    resid, pre_gain, post_gain, w_query, w_key, w_value, w_out, key_cache, value_cache,
    lengths, concept, steer_layer, strength, directions,
):
    rc, W = resid.shape
    R = lengths.shape[0]
    D = pre_gain.shape[1]
    HD = key_cache.shape[-1]
    H = w_query.shape[2] // HD
    KL = key_cache.shape[2]
    G = R // BLOCK
    Wp = -(-(D // 128) // T) * 128
    sper = BLOCK // rc
    dma = pltpu.SemaphoreType.DMA
    vm = pltpu.VMEM
    hbm = pl.BlockSpec(memory_space=pltpu.HBM)
    turned = directions.T
    scratch = [
        pltpu.SMEM((R,), jnp.int32), pltpu.SMEM((R,), jnp.int32), pltpu.SMEM((R,), jnp.int32),
        pltpu.SMEM((R,), f32), vm((rc, W), bf16), vm((1, D), f32), vm((1, D), f32),
        vm(w_query.shape[1:], bf16), vm(w_key.shape[1:], bf16), vm(w_value.shape[1:], bf16),
        vm(w_out.shape[1:], bf16), vm(key_cache.shape[1:], bf16), vm(value_cache.shape[1:], bf16),
        vm(turned.shape, bf16),
        vm((S, T, rc, W), bf16), vm((G, BLOCK, D), bf16), vm((G, BLOCK, D), bf16),
        vm((G, BLOCK, D), f32),
        vm((T, R, W), bf16), vm((R, W), f32), vm((R, HD), f32), vm((R, HD), jnp.int32),
        vm((H, BLOCK, HD), f32), vm((KL, BLOCK, HD), f32), vm((KL, BLOCK, HD), f32),
        vm((BLOCK, H * HD), f32),
        vm((G, BLOCK, D), bf16), vm((G, T, BLOCK, Wp), bf16), vm((G, BLOCK, Wp + 128), bf16),
        vm((G, T, BLOCK, Wp + 128), bf16), vm((BLOCK, Wp), bf16), vm((BLOCK, Wp), bf16),
        vm((T, BLOCK, 128), bf16), vm((BLOCK, Wp), f32),
        dma((14,)), dma((T,)), dma((S, T)), dma((G,)), dma((G,)), dma((T,)), dma((T,)),
        dma((G, T)), dma((G, T)), dma((G, T)), dma((G, T)),
        dma((G, sper)), dma, dma((G, sper)), dma, dma((G, sper * T)), dma((T,)),
    ]
    return pl.pallas_call(
        functools.partial(kernel, S, T),
        out_shape=jax.ShapeDtypeStruct((rc, W), bf16),
        in_specs=[hbm] * 14,
        out_specs=pl.BlockSpec(memory_space=pltpu.VMEM),
        scratch_shapes=scratch,
        compiler_params=pltpu.CompilerParams(
            collective_id=0, has_side_effects=True, vmem_limit_bytes=63 * 1024 * 1024),
    )(lengths, concept, steer_layer, strength, resid, pre_gain, post_gain,
      w_query, w_key, w_value, w_out, key_cache, value_cache, turned)


def solution(mesh):
    placed = (
        P("section", "tensor"),
        P("section", None),
        P("section", None),
        P("section", None, "tensor"),
        P("section", None, "tensor"),
        P("section", None, "tensor"),
        P("section", "tensor", None),
        P("section", None, "tensor", None, None),
        P("section", None, "tensor", None, None),
        P(),
        P(),
        P(),
        P(),
        P(None, "tensor"),
    )
    S, T = mesh.shape["section"], mesh.shape["tensor"]
    return jax.shard_map(
        functools.partial(on_device, S, T), mesh=mesh, in_specs=placed,
        out_specs=P("section", "tensor"), check_vma=False,
    )
```

```python
import functools
import math

import jax
import jax.numpy as jnp
from jax import lax
from jax.experimental import pallas as pl
from jax.experimental.pallas import tpu as pltpu
from jax.sharding import PartitionSpec as P

MESH = pl.DeviceIdType.MESH
epsilon = 1e-06
softcap_limit = 50.0
BLOCK = 16
f32 = jnp.float32
bf16 = jnp.bfloat16


def kernel(
    S, T,
    lengths_h, concept_h, steer_h, strength_h,
    resid_h, pre_h, post_h, wq, wk, wv, wo, kc, vc, dirs,
    out_ref,
    lengths, concept, steer_layer, strength, resid, pre, post,
    wq_v, wk_v, wv_v, wo_v, kc_v, vc_v, dirs_v,
    xg, xprev, x_ref, base, st, dself, gates, lens,
    proj, qs, ks, vs, heads, part, rs, msg, ag, fin_x, fin_p, fin_s, fin_f,
    w_sem, xg_ss, xg_rs, xf_ss, xf_rs, st_ss, st_rs, rs_ss, rs_rs, ag_ss, ag_rs,
    fx_ss, fx_rs, fp_ss, fp_rs, fs_ss, fs_rs,
):
    s = lax.axis_index("section")
    t = lax.axis_index("tensor")
    N = S * T
    G, _, D = x_ref.shape
    R = G * BLOCK
    rc, W = resid.shape
    HD = kc_v.shape[-1]
    CTX = kc_v.shape[2]
    KL = kc_v.shape[1]
    H = qs.shape[0]
    group = H // KL
    chunks = D // 128
    Wp = fin_f.shape[1]
    sper = BLOCK // rc
    per = next(n for n in range(1, T + 1) if (chunks * n) % T == 0)
    quarters = T // per
    GW = chunks * per // T * 128
    my_j = t // per
    last = S - 1
    half = HD // 2
    scale = float(D // (H * T)) ** (-0.5)

    def begin(o):
        return (o * chunks) // T * 128

    def window(o):
        return pl.ds(pl.multiple_of(begin(o), 128), Wp)

    def wait(ref, sem):
        pltpu.make_async_copy(ref, ref, sem).wait()

    def remote(src, dst, ss, rsem, ds, dt):
        return pltpu.make_async_remote_copy(
            src_ref=src, dst_ref=dst, send_sem=ss, recv_sem=rsem,
            device_id=(ds, dt), device_id_type=MESH)

    def send(src, dst, ss, rsem, ds, dt):
        mine = (ds == s) & (dt == t)

        @pl.when(mine)
        def _():
            pltpu.make_async_copy(src, dst, rsem).start()

        @pl.when(jnp.logical_not(mine))
        def _():
            remote(src, dst, ss, rsem, ds, dt).start()

    def sent(src, ss, ds, dt):
        @pl.when(jnp.logical_not((ds == s) & (dt == t)))
        def _():
            wait(src, ss)

    barrier = pltpu.get_barrier_semaphore()
    me = s * T + t

    def greet(n, carry):
        other = lax.rem(me + n, N)
        pl.semaphore_signal(barrier, inc=1, device_id=(other // T, lax.rem(other, T)),
                            device_id_type=MESH)
        return carry

    lax.fori_loop(1, N, greet, 0)

    pairs = [(resid_h, resid), (lengths_h, lengths), (concept_h, concept), (steer_h, steer_layer),
             (strength_h, strength), (pre_h, pre), (post_h, post), (dirs, dirs_v),
             (wq.at[0], wq_v), (wk.at[0], wk_v), (wv.at[0], wv_v), (kc.at[0], kc_v),
             (vc.at[0], vc_v), (wo.at[0], wo_v)]
    loads = [pltpu.make_async_copy(a, b, w_sem.at[i]) for i, (a, b) in enumerate(pairs)]
    for one in loads:
        one.start()
    loads[0].wait()
    pl.semaphore_wait(barrier, N - 1)

    for k in range(T):
        dt = lax.rem(t + k, T)
        send(resid, xg.at[s, t], xg_ss.at[k], xg_rs.at[s, t], 0, dt)

    for n in range(1, 7):
        loads[n].wait()
    rows = lax.broadcasted_iota(jnp.int32, (R, HD), 0)
    zero_i = jnp.zeros((R, HD), jnp.int32)

    def gather(i, carry):
        a, b, c, d = carry
        hit = rows == i
        return (jnp.where(hit, lengths[i], a), jnp.where(hit, concept[i], b),
                jnp.where(hit, steer_layer[i], c), jnp.where(hit, strength[i], d))

    len_v, con_v, lay_v, str_v = lax.fori_loop(
        0, R, gather, (zero_i, zero_i, zero_i, jnp.zeros((R, HD), f32)))
    lens[...] = len_v
    gates[...] = str_v * (lay_v == last).astype(f32)
    lane = lax.broadcasted_iota(jnp.int32, (R, HD), 1)
    frequency = jnp.exp(lax.rem(lane, half).astype(f32) * (-2.0 * math.log(10000.0) / HD))
    angle = len_v.astype(f32) * frequency
    cosine = jnp.cos(angle)
    sine = jnp.sin(angle)
    sine = jnp.where(lane < half, -sine, sine)

    loads[7].wait()
    nc = dirs_v.shape[1]
    one_hot = (con_v[:, 0:1] == lax.broadcasted_iota(jnp.int32, (R, nc), 1)).astype(f32).astype(bf16)
    picked = lax.dot_general(one_hot, dirs_v[...], (((1,), (1,)), ((), ())),
                             preferred_element_type=f32)
    dself[...] = picked

    def matmul(v, part_rows):
        return jnp.concatenate([
            jnp.dot(v, w[part_rows, :], preferred_element_type=f32)
            for w in (wq_v, wk_v, wv_v)], axis=1)

    @pl.when(s == 0)
    def _():
        for a in range(G):
            for n in range(sper):
                owner = a * sper + n
                for b in range(T):
                    wait(xg.at[owner, b], xg_rs.at[owner, b])
                base[a, n * rc:(n + 1) * rc, :] = jnp.concatenate(
                    [xg[owner, b].astype(f32) for b in range(T)], axis=1)
            x_ref[a] = base[a].astype(bf16)
            remote(x_ref.at[a], xprev.at[a], xf_ss.at[a], xf_rs.at[a], s + 1, t).start()

    @pl.when(s > 0)
    def _():
        st[t] = picked.astype(bf16)
        for k in range(T):
            wait(resid, xg_ss.at[k])
        for k in range(1, T):
            dt = lax.rem(t + k, T)
            remote(st.at[t], st.at[t], st_ss.at[k], st_rs.at[t], s, dt).start()
        for k in range(1, T):
            b = lax.rem(t + k, T)
            wait(st.at[b], st_rs.at[b])
        gate = (str_v * (lay_v == s - 1).astype(f32))[:, 0:1]
        full = jnp.concatenate([st[b].astype(f32) for b in range(T)], axis=1)
        for a in range(G):
            cut = slice(a * BLOCK, (a + 1) * BLOCK)
            wait(xprev.at[a], xf_rs.at[a])
            base[a] = xprev[a].astype(f32) + gate[cut] * full[cut]

    for n in (8, 9, 10):
        loads[n].wait()
    proj[...] = matmul(
        jnp.concatenate([(base[a] * pre[...]).astype(bf16) for a in range(G)], axis=0),
        slice(0, D))

    my_cols = window(t)
    span = 8 * CTX
    tiles = BLOCK // 8
    height = tiles * KL * 8 * group
    col = lax.broadcasted_iota(jnp.int32, (height, span), 1)
    row = lax.broadcasted_iota(jnp.int32, (height, span), 0)
    same = (col // CTX) == lax.rem(row, 8)
    spot = lax.rem(col, CTX)
    tail_lane = lax.broadcasted_iota(jnp.int32, (BLOCK, 128), 1)
    piece_lane = lax.broadcasted_iota(jnp.int32, (BLOCK, Wp), 1)
    fresh = piece_lane < begin(t + 1) - begin(t)

    def rope(v, cut):
        return (v * cosine[cut] + pltpu.roll(v, half, 1) * sine[cut]).astype(bf16).astype(f32)

    def total_of(ref, index):
        total = jnp.zeros((BLOCK, 1), f32)
        for o in range(T):
            tail = index(ref, o).astype(f32)
            total = total + tail[:, 0:1] + tail[:, 64:65]
        return lax.rsqrt(total / D + epsilon)

    def enter(a):
        cut = slice(a * BLOCK, (a + 1) * BLOCK)

        @pl.when(s > 0)
        def _():
            acc = None
            for i in range(quarters):
                j = lax.rem(my_j + i, quarters)
                for n in range(per):
                    wait(ag.at[a, j * per + n], ag_rs.at[a, j * per + n])
                p = jnp.concatenate(
                    [ag[a, j * per + n, :, 0:begin(n + 1) - begin(n)].astype(f32)
                     for n in range(per)], axis=1)
                at = pl.ds(pl.multiple_of(j * GW, 128), GW)
                term = matmul((p * pre[:, at]).astype(bf16), at)
                acc = term if acc is None else acc + term
            inv = total_of(ag, lambda ref, o: ref[a, o, :, Wp:Wp + 128])
            for o in range(T):
                lo = begin(o)
                size = begin(o + 1) - lo
                base[a, :, lo:lo + size] = (
                    base[a, :, lo:lo + size] + inv * ag[a, o, :, 0:size].astype(f32))
            x_ref[a] = base[a].astype(bf16)
            proj[cut, :] = proj[cut, :] + inv * acc

        @pl.when((s > 0) & (s < last))
        def _():
            remote(x_ref.at[a], xprev.at[a], xf_ss.at[a], xf_rs.at[a], s + 1, t).start()

        @pl.when(s == last)
        def _():
            for n in range(sper):
                send(x_ref.at[a, :, my_cols], fin_x, fx_ss.at[a, n], fx_rs, a * sper + n, t)

        xf = x_ref[a].astype(f32)
        inv = lax.rsqrt(jnp.mean(xf * xf, axis=1, keepdims=True) + epsilon)
        all_ = proj[cut, :] * inv
        for h in range(H):
            qs[h] = rope(all_[:, h * HD:(h + 1) * HD], cut)
        for h in range(KL):
            c0 = (H + h) * HD
            ks[h] = rope(all_[:, c0:c0 + HD], cut)
            c0 = (H + KL + h) * HD
            vs[h] = all_[:, c0:c0 + HD].astype(bf16).astype(f32)

    def attend(a):
        if a == 0:
            loads[11].wait()
            loads[12].wait()
        units = [(i, h) for i in range(tiles) for h in range(KL)]
        qq = jnp.concatenate([qs[h * group + g, 8 * i:8 * i + 8, :]
                              for i, h in units for g in range(group)], axis=0)
        kk = jnp.concatenate([ks[h, 8 * i:8 * i + 8, :]
                              for i, h in units for g in range(group)], axis=0)
        vv = jnp.concatenate([vs[h, 8 * i:8 * i + 8, :]
                              for i, h in units for g in range(group)], axis=0)
        r0 = a * BLOCK
        limit = jnp.concatenate([lens[r0 + 8 * i:r0 + 8 * i + 8, 0:1]
                                 for i, h in units for g in range(group)], axis=0)
        qb = qq.astype(bf16)
        step = 8 * group
        scores = jnp.concatenate([
            lax.dot_general(qb[n * step:(n + 1) * step],
                            kc_v[r0 + 8 * i:r0 + 8 * i + 8, h].reshape(span, HD),
                            (((1,), (1,)), ((), ())), preferred_element_type=f32)
            for n, (i, h) in enumerate(units)], axis=0) * scale
        own = jnp.sum(qq * kk, axis=1, keepdims=True) * scale
        weight = jnp.where(
            same & (spot < limit),
            jnp.exp(softcap_limit * jnp.tanh(scores / softcap_limit) - softcap_limit), 0.0)
        own_w = jnp.exp(softcap_limit * jnp.tanh(own / softcap_limit) - softcap_limit)
        total = jnp.sum(weight, axis=1, keepdims=True) + own_w
        probs = (weight / total).astype(bf16)
        own_p = (own_w / total).astype(bf16).astype(f32)
        mixed = jnp.concatenate([
            jnp.dot(probs[n * step:(n + 1) * step],
                    vc_v[r0 + 8 * i:r0 + 8 * i + 8, h].reshape(span, HD),
                    preferred_element_type=f32)
            for n, (i, h) in enumerate(units)], axis=0) + own_p * vv
        for n, (i, h) in enumerate(units):
            for g in range(group):
                c0 = (h * group + g) * HD
                heads[8 * i:8 * i + 8, c0:c0 + HD] = mixed[n * step + 8 * g:n * step + 8 * g + 8, :]

    def targets():
        k = 0
        for i in list(range(1, quarters)) + [0]:
            j = lax.rem(my_j + i, quarters)
            outs = []
            for n in range(per if i else per - 1):
                k += 1
                inner = n if i else lax.rem(lax.rem(t, per) + n + 1, per)
                outs.append((j * per + inner, k))
            yield j, outs

    def leave(a):
        if a == 0:
            loads[13].wait()
        hb = heads[...].astype(bf16)
        for j, outs in targets():
            at = pl.ds(pl.multiple_of(j * GW, 128), GW)
            part[a, :, at] = jnp.dot(hb, wo_v[:, at], preferred_element_type=f32).astype(bf16)
            for o, k in outs:
                remote(part.at[a, :, window(o)], rs.at[a, t], rs_ss.at[a, k], rs_rs.at[a, t],
                       s, o).start()
        rs[a, t] = part[a, :, my_cols]

    def reduce(a):
        for k in range(1, T):
            o = lax.rem(t + k, T)
            wait(rs.at[a, o], rs_rs.at[a, o])
        summed = jnp.zeros((BLOCK, Wp), f32)
        for o in range(T):
            summed = summed + rs[a, o].astype(f32)
        squares = jnp.sum(jnp.where(fresh, summed * summed, 0.0), axis=1, keepdims=True)
        high = squares.astype(bf16).astype(f32)
        msg[a, :, 0:Wp] = (summed * post[:, my_cols]).astype(bf16)
        msg[a, :, Wp:Wp + 128] = jnp.where(tail_lane < 64, high, squares - high).astype(bf16)

        @pl.when(s < last)
        def _():
            for k in range(T):
                dt = lax.rem(t + k, T)
                remote(msg.at[a], ag.at[a, t], ag_ss.at[a, k], ag_rs.at[a, t], s + 1, dt).start()

        @pl.when(s == last)
        def _():
            for n in range(sper):
                ds = a * sper + n
                send(msg.at[a, :, pl.ds(0, Wp)], fin_p, fp_ss.at[a, n], fp_rs, ds, t)
                for b in range(T):
                    send(msg.at[a, :, pl.ds(Wp, 128)], fin_s.at[t], fs_ss.at[a, n * T + b],
                         fs_rs.at[t], ds, b)

    for a in range(G):
        enter(a)
        if a > 0:
            reduce(a - 1)
        attend(a)
        leave(a)
    reduce(G - 1)

    wait(fin_x, fx_rs)
    wait(fin_p, fp_rs)
    for o in range(T):
        wait(fin_s.at[o], fs_rs.at[o])
    inv = total_of(fin_s, lambda ref, o: ref[o])
    fin_f[...] = fin_x[...].astype(f32) + inv * fin_p[...].astype(f32)
    here = fin_f[pl.ds(pl.multiple_of(lax.rem(s, sper) * rc, rc), rc), :]
    shift = t * W - begin(t)
    piece = here[:, 0:W]
    for b in sorted({(p * W) % 128 for p in range(T)} - {0}):
        piece = jnp.where(shift == b, here[:, b:b + W], piece)
    own_rows = pl.ds(pl.multiple_of(s * rc, rc), rc)
    out_ref[...] = (piece + gates[own_rows, :][:, 0:1] * dself[own_rows, :]).astype(bf16)

    @pl.when(s == 0)
    def _():
        for k in range(1, T):
            wait(resid, xg_ss.at[k])

    for a in range(G):
        for j, outs in targets():
            for o, k in outs:
                wait(part.at[a, :, window(o)], rs_ss.at[a, k])

    @pl.when(s > 0)
    def _():
        for k in range(1, T):
            wait(st.at[t], st_ss.at[k])

    @pl.when(s < last)
    def _():
        for a in range(G):
            wait(x_ref.at[a], xf_ss.at[a])
            for k in range(T):
                wait(msg.at[a], ag_ss.at[a, k])

    @pl.when(s == last)
    def _():
        for a in range(G):
            for n in range(sper):
                ds = a * sper + n
                sent(x_ref.at[a, :, my_cols], fx_ss.at[a, n], ds, t)
                sent(msg.at[a, :, pl.ds(0, Wp)], fp_ss.at[a, n], ds, t)
                for b in range(T):
                    sent(msg.at[a, :, pl.ds(Wp, 128)], fs_ss.at[a, n * T + b], ds, b)


def on_device(
    S, T,
    resid, pre_gain, post_gain, w_query, w_key, w_value, w_out, key_cache, value_cache,
    lengths, concept, steer_layer, strength, directions,
):
    rc, W = resid.shape
    R = lengths.shape[0]
    D = pre_gain.shape[1]
    HD = key_cache.shape[-1]
    H = w_query.shape[2] // HD
    KL = key_cache.shape[2]
    G = R // BLOCK
    Wp = -(-(D // 128) // T) * 128
    sper = BLOCK // rc
    dma = pltpu.SemaphoreType.DMA
    vm = pltpu.VMEM
    hbm = pl.BlockSpec(memory_space=pltpu.HBM)
    turned = directions.T
    scratch = [
        pltpu.SMEM((R,), jnp.int32), pltpu.SMEM((R,), jnp.int32), pltpu.SMEM((R,), jnp.int32),
        pltpu.SMEM((R,), f32), vm((rc, W), bf16), vm((1, D), f32), vm((1, D), f32),
        vm(w_query.shape[1:], bf16), vm(w_key.shape[1:], bf16), vm(w_value.shape[1:], bf16),
        vm(w_out.shape[1:], bf16), vm(key_cache.shape[1:], bf16), vm(value_cache.shape[1:], bf16),
        vm(turned.shape, bf16),
        vm((S, T, rc, W), bf16), vm((G, BLOCK, D), bf16), vm((G, BLOCK, D), bf16),
        vm((G, BLOCK, D), f32),
        vm((T, R, W), bf16), vm((R, W), f32), vm((R, HD), f32), vm((R, HD), jnp.int32),
        vm((R, (H + 2 * KL) * HD), f32),
        vm((H, BLOCK, HD), f32), vm((KL, BLOCK, HD), f32), vm((KL, BLOCK, HD), f32),
        vm((BLOCK, H * HD), f32),
        vm((G, BLOCK, D), bf16), vm((G, T, BLOCK, Wp), bf16), vm((G, BLOCK, Wp + 128), bf16),
        vm((G, T, BLOCK, Wp + 128), bf16), vm((BLOCK, Wp), bf16), vm((BLOCK, Wp), bf16),
        vm((T, BLOCK, 128), bf16), vm((BLOCK, Wp), f32),
        dma((14,)), dma((T,)), dma((S, T)), dma((G,)), dma((G,)), dma((T,)), dma((T,)),
        dma((G, T)), dma((G, T)), dma((G, T)), dma((G, T)),
        dma((G, sper)), dma, dma((G, sper)), dma, dma((G, sper * T)), dma((T,)),
    ]
    return pl.pallas_call(
        functools.partial(kernel, S, T),
        out_shape=jax.ShapeDtypeStruct((rc, W), bf16),
        in_specs=[hbm] * 14,
        out_specs=pl.BlockSpec(memory_space=pltpu.VMEM),
        scratch_shapes=scratch,
        compiler_params=pltpu.CompilerParams(
            collective_id=0, has_side_effects=True, vmem_limit_bytes=63 * 1024 * 1024),
    )(lengths, concept, steer_layer, strength, resid, pre_gain, post_gain,
      w_query, w_key, w_value, w_out, key_cache, value_cache, turned)


def solution(mesh):
    placed = (
        P("section", "tensor"),
        P("section", None),
        P("section", None),
        P("section", None, "tensor"),
        P("section", None, "tensor"),
        P("section", None, "tensor"),
        P("section", "tensor", None),
        P("section", None, "tensor", None, None),
        P("section", None, "tensor", None, None),
        P(),
        P(),
        P(),
        P(),
        P(None, "tensor"),
    )
    S, T = mesh.shape["section"], mesh.shape["tensor"]
    return jax.shard_map(
        functools.partial(on_device, S, T), mesh=mesh, in_specs=placed,
        out_specs=P("section", "tensor"), check_vma=False,
    )
```

```python
import functools
import math

import jax
import jax.numpy as jnp
from jax import lax
from jax.experimental import pallas as pl
from jax.experimental.pallas import tpu as pltpu
from jax.sharding import PartitionSpec as P

MESH = pl.DeviceIdType.MESH
epsilon = 1e-06
softcap_limit = 50.0
BLOCK = 32
f32 = jnp.float32
bf16 = jnp.bfloat16


def kernel(
    S, T,
    lengths_h, concept_h, steer_h, strength_h,
    resid_h, pre_h, post_h, wq, wk, wv, wo, kc, vc, dirs,
    out_ref,
    lengths, concept, steer_layer, strength, resid, pre, post,
    wq_v, wk_v, wv_v, wo_v, kc_v, vc_v, dirs_v,
    xg, xprev, x_ref, base, st, dself, gates, lens,
    proj, qs, ks, vs, heads, part, rs, msg, ag, fin_x, fin_p, fin_s, fin_f,
    w_sem, xg_ss, xg_rs, xf_ss, xf_rs, st_ss, st_rs, rs_ss, rs_rs, ag_ss, ag_rs,
    fx_ss, fx_rs, fp_ss, fp_rs, fs_ss, fs_rs,
):
    s = lax.axis_index("section")
    t = lax.axis_index("tensor")
    N = S * T
    G, _, D = x_ref.shape
    R = G * BLOCK
    rc, W = resid.shape
    HD = kc_v.shape[-1]
    CTX = kc_v.shape[2]
    KL = kc_v.shape[1]
    H = qs.shape[0]
    group = H // KL
    chunks = D // 128
    Wp = fin_f.shape[1]
    sper = BLOCK // rc
    per = next(n for n in range(1, T + 1) if (chunks * n) % T == 0)
    quarters = T // per
    GW = chunks * per // T * 128
    my_j = t // per
    last = S - 1
    half = HD // 2
    scale = float(D // (H * T)) ** (-0.5)

    def begin(o):
        return (o * chunks) // T * 128

    def window(o):
        return pl.ds(pl.multiple_of(begin(o), 128), Wp)

    def wait(ref, sem):
        pltpu.make_async_copy(ref, ref, sem).wait()

    def remote(src, dst, ss, rsem, ds, dt):
        return pltpu.make_async_remote_copy(
            src_ref=src, dst_ref=dst, send_sem=ss, recv_sem=rsem,
            device_id=(ds, dt), device_id_type=MESH)

    def send(src, dst, ss, rsem, ds, dt):
        mine = (ds == s) & (dt == t)

        @pl.when(mine)
        def _():
            pltpu.make_async_copy(src, dst, rsem).start()

        @pl.when(jnp.logical_not(mine))
        def _():
            remote(src, dst, ss, rsem, ds, dt).start()

    def sent(src, ss, ds, dt):
        @pl.when(jnp.logical_not((ds == s) & (dt == t)))
        def _():
            wait(src, ss)

    barrier = pltpu.get_barrier_semaphore()
    me = s * T + t

    def greet(n, carry):
        other = lax.rem(me + n, N)
        pl.semaphore_signal(barrier, inc=1, device_id=(other // T, lax.rem(other, T)),
                            device_id_type=MESH)
        return carry

    lax.fori_loop(1, N, greet, 0)

    pairs = [(resid_h, resid), (lengths_h, lengths), (concept_h, concept), (steer_h, steer_layer),
             (strength_h, strength), (pre_h, pre), (post_h, post), (dirs, dirs_v),
             (wq.at[0], wq_v), (wk.at[0], wk_v), (wv.at[0], wv_v), (kc.at[0], kc_v),
             (vc.at[0], vc_v), (wo.at[0], wo_v)]
    loads = [pltpu.make_async_copy(a, b, w_sem.at[i]) for i, (a, b) in enumerate(pairs)]
    for one in loads:
        one.start()
    loads[0].wait()
    pl.semaphore_wait(barrier, N - 1)

    for k in range(T):
        dt = lax.rem(t + k, T)
        send(resid, xg.at[s, t], xg_ss.at[k], xg_rs.at[s, t], 0, dt)

    for n in range(1, 7):
        loads[n].wait()
    rows = lax.broadcasted_iota(jnp.int32, (R, HD), 0)
    zero_i = jnp.zeros((R, HD), jnp.int32)

    def gather(i, carry):
        a, b, c, d = carry
        hit = rows == i
        return (jnp.where(hit, lengths[i], a), jnp.where(hit, concept[i], b),
                jnp.where(hit, steer_layer[i], c), jnp.where(hit, strength[i], d))

    len_v, con_v, lay_v, str_v = lax.fori_loop(
        0, R, gather, (zero_i, zero_i, zero_i, jnp.zeros((R, HD), f32)))
    lens[...] = len_v
    gates[...] = str_v * (lay_v == last).astype(f32)
    lane = lax.broadcasted_iota(jnp.int32, (R, HD), 1)
    frequency = jnp.exp(lax.rem(lane, half).astype(f32) * (-2.0 * math.log(10000.0) / HD))
    angle = len_v.astype(f32) * frequency
    cosine = jnp.cos(angle)
    sine = jnp.sin(angle)
    sine = jnp.where(lane < half, -sine, sine)

    loads[7].wait()
    nc = dirs_v.shape[1]
    one_hot = (con_v[:, 0:1] == lax.broadcasted_iota(jnp.int32, (R, nc), 1)).astype(f32).astype(bf16)
    picked = lax.dot_general(one_hot, dirs_v[...], (((1,), (1,)), ((), ())),
                             preferred_element_type=f32)
    dself[...] = picked

    def matmul(v, part_rows):
        return jnp.concatenate([
            jnp.dot(v, w[part_rows, :], preferred_element_type=f32)
            for w in (wq_v, wk_v, wv_v)], axis=1)

    @pl.when(s == 0)
    def _():
        for a in range(G):
            for n in range(sper):
                owner = a * sper + n
                for b in range(T):
                    wait(xg.at[owner, b], xg_rs.at[owner, b])
                base[a, n * rc:(n + 1) * rc, :] = jnp.concatenate(
                    [xg[owner, b].astype(f32) for b in range(T)], axis=1)
            x_ref[a] = base[a].astype(bf16)
            remote(x_ref.at[a], xprev.at[a], xf_ss.at[a], xf_rs.at[a], s + 1, t).start()

    @pl.when(s > 0)
    def _():
        st[t] = picked.astype(bf16)
        for k in range(T):
            wait(resid, xg_ss.at[k])
        for k in range(1, T):
            dt = lax.rem(t + k, T)
            remote(st.at[t], st.at[t], st_ss.at[k], st_rs.at[t], s, dt).start()
        for k in range(1, T):
            b = lax.rem(t + k, T)
            wait(st.at[b], st_rs.at[b])
        gate = (str_v * (lay_v == s - 1).astype(f32))[:, 0:1]
        full = jnp.concatenate([st[b].astype(f32) for b in range(T)], axis=1)
        for a in range(G):
            cut = slice(a * BLOCK, (a + 1) * BLOCK)
            wait(xprev.at[a], xf_rs.at[a])
            base[a] = xprev[a].astype(f32) + gate[cut] * full[cut]

    for n in (8, 9, 10):
        loads[n].wait()
    proj[...] = matmul(
        jnp.concatenate([(base[a] * pre[...]).astype(bf16) for a in range(G)], axis=0),
        slice(0, D))

    my_cols = window(t)
    span = 8 * CTX
    tiles = BLOCK // 8
    height = tiles * KL * 8 * group
    col = lax.broadcasted_iota(jnp.int32, (height, span), 1)
    row = lax.broadcasted_iota(jnp.int32, (height, span), 0)
    same = (col // CTX) == lax.rem(row, 8)
    spot = lax.rem(col, CTX)
    tail_lane = lax.broadcasted_iota(jnp.int32, (BLOCK, 128), 1)
    piece_lane = lax.broadcasted_iota(jnp.int32, (BLOCK, Wp), 1)
    fresh = piece_lane < begin(t + 1) - begin(t)

    def rope(v, cut):
        return (v * cosine[cut] + pltpu.roll(v, half, 1) * sine[cut]).astype(bf16).astype(f32)

    def total_of(ref, index):
        total = jnp.zeros((BLOCK, 1), f32)
        for o in range(T):
            tail = index(ref, o).astype(f32)
            total = total + tail[:, 0:1] + tail[:, 64:65]
        return lax.rsqrt(total / D + epsilon)

    def enter(a):
        cut = slice(a * BLOCK, (a + 1) * BLOCK)

        @pl.when(s > 0)
        def _():
            acc = None
            for i in range(quarters):
                j = lax.rem(my_j + i, quarters)
                for n in range(per):
                    wait(ag.at[a, j * per + n], ag_rs.at[a, j * per + n])
                p = jnp.concatenate(
                    [ag[a, j * per + n, :, 0:begin(n + 1) - begin(n)].astype(f32)
                     for n in range(per)], axis=1)
                at = pl.ds(pl.multiple_of(j * GW, 128), GW)
                term = matmul((p * pre[:, at]).astype(bf16), at)
                acc = term if acc is None else acc + term
            inv = total_of(ag, lambda ref, o: ref[a, o, :, Wp:Wp + 128])
            for o in range(T):
                lo = begin(o)
                size = begin(o + 1) - lo
                base[a, :, lo:lo + size] = (
                    base[a, :, lo:lo + size] + inv * ag[a, o, :, 0:size].astype(f32))
            x_ref[a] = base[a].astype(bf16)
            proj[cut, :] = proj[cut, :] + inv * acc

        @pl.when((s > 0) & (s < last))
        def _():
            remote(x_ref.at[a], xprev.at[a], xf_ss.at[a], xf_rs.at[a], s + 1, t).start()

        @pl.when(s == last)
        def _():
            for n in range(sper):
                send(x_ref.at[a, :, my_cols], fin_x, fx_ss.at[a, n], fx_rs, a * sper + n, t)

        xf = x_ref[a].astype(f32)
        inv = lax.rsqrt(jnp.mean(xf * xf, axis=1, keepdims=True) + epsilon)
        all_ = proj[cut, :] * inv
        for h in range(H):
            qs[h] = rope(all_[:, h * HD:(h + 1) * HD], cut)
        for h in range(KL):
            c0 = (H + h) * HD
            ks[h] = rope(all_[:, c0:c0 + HD], cut)
            c0 = (H + KL + h) * HD
            vs[h] = all_[:, c0:c0 + HD].astype(bf16).astype(f32)

    def attend(a):
        if a == 0:
            loads[11].wait()
            loads[12].wait()
        units = [(i, h) for i in range(tiles) for h in range(KL)]
        qq = jnp.concatenate([qs[h * group + g, 8 * i:8 * i + 8, :]
                              for i, h in units for g in range(group)], axis=0)
        kk = jnp.concatenate([ks[h, 8 * i:8 * i + 8, :]
                              for i, h in units for g in range(group)], axis=0)
        vv = jnp.concatenate([vs[h, 8 * i:8 * i + 8, :]
                              for i, h in units for g in range(group)], axis=0)
        r0 = a * BLOCK
        limit = jnp.concatenate([lens[r0 + 8 * i:r0 + 8 * i + 8, 0:1]
                                 for i, h in units for g in range(group)], axis=0)
        qb = qq.astype(bf16)
        step = 8 * group
        scores = jnp.concatenate([
            lax.dot_general(qb[n * step:(n + 1) * step],
                            kc_v[r0 + 8 * i:r0 + 8 * i + 8, h].reshape(span, HD),
                            (((1,), (1,)), ((), ())), preferred_element_type=f32)
            for n, (i, h) in enumerate(units)], axis=0) * scale
        own = jnp.sum(qq * kk, axis=1, keepdims=True) * scale
        weight = jnp.where(
            same & (spot < limit),
            jnp.exp(softcap_limit * jnp.tanh(scores / softcap_limit) - softcap_limit), 0.0)
        own_w = jnp.exp(softcap_limit * jnp.tanh(own / softcap_limit) - softcap_limit)
        total = jnp.sum(weight, axis=1, keepdims=True) + own_w
        probs = (weight / total).astype(bf16)
        own_p = (own_w / total).astype(bf16).astype(f32)
        mixed = jnp.concatenate([
            jnp.dot(probs[n * step:(n + 1) * step],
                    vc_v[r0 + 8 * i:r0 + 8 * i + 8, h].reshape(span, HD),
                    preferred_element_type=f32)
            for n, (i, h) in enumerate(units)], axis=0) + own_p * vv
        for n, (i, h) in enumerate(units):
            for g in range(group):
                c0 = (h * group + g) * HD
                heads[8 * i:8 * i + 8, c0:c0 + HD] = mixed[n * step + 8 * g:n * step + 8 * g + 8, :]

    def targets():
        k = 0
        for i in list(range(1, quarters)) + [0]:
            j = lax.rem(my_j + i, quarters)
            outs = []
            for n in range(per if i else per - 1):
                k += 1
                inner = n if i else lax.rem(lax.rem(t, per) + n + 1, per)
                outs.append((j * per + inner, k))
            yield j, outs

    def leave(a):
        if a == 0:
            loads[13].wait()
        hb = heads[...].astype(bf16)
        for j, outs in targets():
            at = pl.ds(pl.multiple_of(j * GW, 128), GW)
            part[a, :, at] = jnp.dot(hb, wo_v[:, at], preferred_element_type=f32).astype(bf16)
            for o, k in outs:
                remote(part.at[a, :, window(o)], rs.at[a, t], rs_ss.at[a, k], rs_rs.at[a, t],
                       s, o).start()
        rs[a, t] = part[a, :, my_cols]

    def reduce(a):
        for k in range(1, T):
            o = lax.rem(t + k, T)
            wait(rs.at[a, o], rs_rs.at[a, o])
        summed = jnp.zeros((BLOCK, Wp), f32)
        for o in range(T):
            summed = summed + rs[a, o].astype(f32)
        squares = jnp.sum(jnp.where(fresh, summed * summed, 0.0), axis=1, keepdims=True)
        high = squares.astype(bf16).astype(f32)
        msg[a, :, 0:Wp] = (summed * post[:, my_cols]).astype(bf16)
        msg[a, :, Wp:Wp + 128] = jnp.where(tail_lane < 64, high, squares - high).astype(bf16)

        @pl.when(s < last)
        def _():
            for k in range(T):
                dt = lax.rem(t + k, T)
                remote(msg.at[a], ag.at[a, t], ag_ss.at[a, k], ag_rs.at[a, t], s + 1, dt).start()

        @pl.when(s == last)
        def _():
            for n in range(sper):
                ds = a * sper + n
                send(msg.at[a, :, pl.ds(0, Wp)], fin_p, fp_ss.at[a, n], fp_rs, ds, t)
                for b in range(T):
                    send(msg.at[a, :, pl.ds(Wp, 128)], fin_s.at[t], fs_ss.at[a, n * T + b],
                         fs_rs.at[t], ds, b)

    for a in range(G):
        enter(a)
        if a > 0:
            reduce(a - 1)
        attend(a)
        leave(a)
    reduce(G - 1)

    wait(fin_x, fx_rs)
    wait(fin_p, fp_rs)
    for o in range(T):
        wait(fin_s.at[o], fs_rs.at[o])
    inv = total_of(fin_s, lambda ref, o: ref[o])
    fin_f[...] = fin_x[...].astype(f32) + inv * fin_p[...].astype(f32)
    here = fin_f[pl.ds(pl.multiple_of(lax.rem(s, sper) * rc, rc), rc), :]
    shift = t * W - begin(t)
    piece = here[:, 0:W]
    for b in sorted({(p * W) % 128 for p in range(T)} - {0}):
        piece = jnp.where(shift == b, here[:, b:b + W], piece)
    own_rows = pl.ds(pl.multiple_of(s * rc, rc), rc)
    out_ref[...] = (piece + gates[own_rows, :][:, 0:1] * dself[own_rows, :]).astype(bf16)

    @pl.when(s == 0)
    def _():
        for k in range(1, T):
            wait(resid, xg_ss.at[k])

    for a in range(G):
        for j, outs in targets():
            for o, k in outs:
                wait(part.at[a, :, window(o)], rs_ss.at[a, k])

    @pl.when(s > 0)
    def _():
        for k in range(1, T):
            wait(st.at[t], st_ss.at[k])

    @pl.when(s < last)
    def _():
        for a in range(G):
            wait(x_ref.at[a], xf_ss.at[a])
            for k in range(T):
                wait(msg.at[a], ag_ss.at[a, k])

    @pl.when(s == last)
    def _():
        for a in range(G):
            for n in range(sper):
                ds = a * sper + n
                sent(x_ref.at[a, :, my_cols], fx_ss.at[a, n], ds, t)
                sent(msg.at[a, :, pl.ds(0, Wp)], fp_ss.at[a, n], ds, t)
                for b in range(T):
                    sent(msg.at[a, :, pl.ds(Wp, 128)], fs_ss.at[a, n * T + b], ds, b)


def on_device(
    S, T,
    resid, pre_gain, post_gain, w_query, w_key, w_value, w_out, key_cache, value_cache,
    lengths, concept, steer_layer, strength, directions,
):
    rc, W = resid.shape
    R = lengths.shape[0]
    D = pre_gain.shape[1]
    HD = key_cache.shape[-1]
    H = w_query.shape[2] // HD
    KL = key_cache.shape[2]
    G = R // BLOCK
    Wp = -(-(D // 128) // T) * 128
    sper = BLOCK // rc
    dma = pltpu.SemaphoreType.DMA
    vm = pltpu.VMEM
    hbm = pl.BlockSpec(memory_space=pltpu.HBM)
    turned = directions.T
    scratch = [
        pltpu.SMEM((R,), jnp.int32), pltpu.SMEM((R,), jnp.int32), pltpu.SMEM((R,), jnp.int32),
        pltpu.SMEM((R,), f32), vm((rc, W), bf16), vm((1, D), f32), vm((1, D), f32),
        vm(w_query.shape[1:], bf16), vm(w_key.shape[1:], bf16), vm(w_value.shape[1:], bf16),
        vm(w_out.shape[1:], bf16), vm(key_cache.shape[1:], bf16), vm(value_cache.shape[1:], bf16),
        vm(turned.shape, bf16),
        vm((S, T, rc, W), bf16), vm((G, BLOCK, D), bf16), vm((G, BLOCK, D), bf16),
        vm((G, BLOCK, D), f32),
        vm((T, R, W), bf16), vm((R, W), f32), vm((R, HD), f32), vm((R, HD), jnp.int32),
        vm((R, (H + 2 * KL) * HD), f32),
        vm((H, BLOCK, HD), f32), vm((KL, BLOCK, HD), f32), vm((KL, BLOCK, HD), f32),
        vm((BLOCK, H * HD), f32),
        vm((G, BLOCK, D), bf16), vm((G, T, BLOCK, Wp), bf16), vm((G, BLOCK, Wp + 128), bf16),
        vm((G, T, BLOCK, Wp + 128), bf16), vm((BLOCK, Wp), bf16), vm((BLOCK, Wp), bf16),
        vm((T, BLOCK, 128), bf16), vm((BLOCK, Wp), f32),
        dma((14,)), dma((T,)), dma((S, T)), dma((G,)), dma((G,)), dma((T,)), dma((T,)),
        dma((G, T)), dma((G, T)), dma((G, T)), dma((G, T)),
        dma((G, sper)), dma, dma((G, sper)), dma, dma((G, sper * T)), dma((T,)),
    ]
    return pl.pallas_call(
        functools.partial(kernel, S, T),
        out_shape=jax.ShapeDtypeStruct((rc, W), bf16),
        in_specs=[hbm] * 14,
        out_specs=pl.BlockSpec(memory_space=pltpu.VMEM),
        scratch_shapes=scratch,
        compiler_params=pltpu.CompilerParams(
            collective_id=0, has_side_effects=True, vmem_limit_bytes=63 * 1024 * 1024),
    )(lengths, concept, steer_layer, strength, resid, pre_gain, post_gain,
      w_query, w_key, w_value, w_out, key_cache, value_cache, turned)


def solution(mesh):
    placed = (
        P("section", "tensor"),
        P("section", None),
        P("section", None),
        P("section", None, "tensor"),
        P("section", None, "tensor"),
        P("section", None, "tensor"),
        P("section", "tensor", None),
        P("section", None, "tensor", None, None),
        P("section", None, "tensor", None, None),
        P(),
        P(),
        P(),
        P(),
        P(None, "tensor"),
    )
    S, T = mesh.shape["section"], mesh.shape["tensor"]
    return jax.shard_map(
        functools.partial(on_device, S, T), mesh=mesh, in_specs=placed,
        out_specs=P("section", "tensor"), check_vma=False,
    )
```

```python
import functools
import math

import jax
import jax.numpy as jnp
from jax import lax
from jax.experimental import pallas as pl
from jax.experimental.pallas import tpu as pltpu
from jax.sharding import PartitionSpec as P

MESH = pl.DeviceIdType.MESH
epsilon = 1e-06
softcap_limit = 50.0
BLOCK = 16
f32 = jnp.float32
bf16 = jnp.bfloat16


def kernel(
    S, T,
    lengths_h, concept_h, steer_h, strength_h,
    resid_h, pre_h, post_h, wq, wk, wv, wo, kc, vc, dirs,
    out_ref,
    lengths, concept, steer_layer, strength, resid, pre, post,
    wq_v, wk_v, wv_v, wo_v, kc_v, vc_v, dirs_v,
    xg, xprev, x_ref, base, st, dself, gates, lens,
    proj, qs, ks, vs, heads, part, rs, msg, ag, fin_x, fin_p, fin_s, fin_f,
    w_sem, xg_ss, xg_rs, xf_ss, xf_rs, st_ss, st_rs, rs_ss, rs_rs, ag_ss, ag_rs,
    fx_ss, fx_rs, fp_ss, fp_rs, fs_ss, fs_rs,
):
    s = lax.axis_index("section")
    t = lax.axis_index("tensor")
    N = S * T
    G, _, D = x_ref.shape
    R = G * BLOCK
    rc, W = resid.shape
    HD = kc_v.shape[-1]
    CTX = kc_v.shape[2]
    KL = kc_v.shape[1]
    H = qs.shape[0]
    group = H // KL
    chunks = D // 128
    Wp = fin_f.shape[1]
    sper = BLOCK // rc
    per = next(n for n in range(1, T + 1) if (chunks * n) % T == 0)
    quarters = T // per
    GW = chunks * per // T * 128
    last = S - 1
    half = HD // 2
    scale = float(D // (H * T)) ** (-0.5)

    def begin(o):
        return (o * chunks) // T * 128

    def window(o):
        return pl.ds(pl.multiple_of(begin(o), 128), Wp)

    def wait(ref, sem):
        pltpu.make_async_copy(ref, ref, sem).wait()

    def remote(src, dst, ss, rsem, ds, dt):
        return pltpu.make_async_remote_copy(
            src_ref=src, dst_ref=dst, send_sem=ss, recv_sem=rsem,
            device_id=(ds, dt), device_id_type=MESH)

    def send(src, dst, ss, rsem, ds, dt):
        mine = (ds == s) & (dt == t)

        @pl.when(mine)
        def _():
            pltpu.make_async_copy(src, dst, rsem).start()

        @pl.when(jnp.logical_not(mine))
        def _():
            remote(src, dst, ss, rsem, ds, dt).start()

    def sent(src, ss, ds, dt):
        @pl.when(jnp.logical_not((ds == s) & (dt == t)))
        def _():
            wait(src, ss)

    barrier = pltpu.get_barrier_semaphore()
    me = s * T + t

    def greet(n, carry):
        other = lax.rem(me + n, N)
        pl.semaphore_signal(barrier, inc=1, device_id=(other // T, lax.rem(other, T)),
                            device_id_type=MESH)
        return carry

    lax.fori_loop(1, N, greet, 0)

    pairs = [(resid_h, resid), (lengths_h, lengths), (concept_h, concept), (steer_h, steer_layer),
             (strength_h, strength), (pre_h, pre), (post_h, post), (dirs, dirs_v),
             (wq.at[0], wq_v), (wk.at[0], wk_v), (wv.at[0], wv_v), (kc.at[0], kc_v),
             (vc.at[0], vc_v), (wo.at[0], wo_v)]
    loads = [pltpu.make_async_copy(a, b, w_sem.at[i]) for i, (a, b) in enumerate(pairs)]
    for one in loads:
        one.start()
    loads[0].wait()
    pl.semaphore_wait(barrier, N - 1)

    for k in range(T):
        dt = lax.rem(t + k, T)
        send(resid, xg.at[s, t], xg_ss.at[k], xg_rs.at[s, t], 0, dt)

    for n in range(1, 7):
        loads[n].wait()
    rows = lax.broadcasted_iota(jnp.int32, (R, HD), 0)
    zero_i = jnp.zeros((R, HD), jnp.int32)

    def gather(i, carry):
        a, b, c, d = carry
        hit = rows == i
        return (jnp.where(hit, lengths[i], a), jnp.where(hit, concept[i], b),
                jnp.where(hit, steer_layer[i], c), jnp.where(hit, strength[i], d))

    len_v, con_v, lay_v, str_v = lax.fori_loop(
        0, R, gather, (zero_i, zero_i, zero_i, jnp.zeros((R, HD), f32)))
    lens[...] = len_v
    gates[...] = str_v * (lay_v == last).astype(f32)
    lane = lax.broadcasted_iota(jnp.int32, (R, HD), 1)
    frequency = jnp.exp(lax.rem(lane, half).astype(f32) * (-2.0 * math.log(10000.0) / HD))
    angle = len_v.astype(f32) * frequency
    cosine = jnp.cos(angle)
    sine = jnp.sin(angle)
    sine = jnp.where(lane < half, -sine, sine)

    loads[7].wait()
    nc = dirs_v.shape[1]
    one_hot = (con_v[:, 0:1] == lax.broadcasted_iota(jnp.int32, (R, nc), 1)).astype(f32).astype(bf16)
    picked = lax.dot_general(one_hot, dirs_v[...], (((1,), (1,)), ((), ())),
                             preferred_element_type=f32)
    dself[...] = picked

    def matmul(v, part_rows):
        return jnp.concatenate([
            jnp.dot(v, w[part_rows, :], preferred_element_type=f32)
            for w in (wq_v, wk_v, wv_v)], axis=1)

    @pl.when(s == 0)
    def _():
        for a in range(G):
            for n in range(sper):
                owner = a * sper + n
                for b in range(T):
                    wait(xg.at[owner, b], xg_rs.at[owner, b])
                base[a, n * rc:(n + 1) * rc, :] = jnp.concatenate(
                    [xg[owner, b].astype(f32) for b in range(T)], axis=1)
            x_ref[a] = base[a].astype(bf16)
            remote(x_ref.at[a], xprev.at[a], xf_ss.at[a], xf_rs.at[a], s + 1, t).start()

    @pl.when(s > 0)
    def _():
        st[t] = picked.astype(bf16)
        for k in range(T):
            wait(resid, xg_ss.at[k])
        for k in range(1, T):
            dt = lax.rem(t + k, T)
            remote(st.at[t], st.at[t], st_ss.at[k], st_rs.at[t], s, dt).start()
        for k in range(1, T):
            b = lax.rem(t + k, T)
            wait(st.at[b], st_rs.at[b])
        gate = (str_v * (lay_v == s - 1).astype(f32))[:, 0:1]
        full = jnp.concatenate([st[b].astype(f32) for b in range(T)], axis=1)
        for a in range(G):
            cut = slice(a * BLOCK, (a + 1) * BLOCK)
            wait(xprev.at[a], xf_rs.at[a])
            base[a] = xprev[a].astype(f32) + gate[cut] * full[cut]

    for n in (8, 9, 10):
        loads[n].wait()
    proj[...] = matmul(
        jnp.concatenate([(base[a] * pre[...]).astype(bf16) for a in range(G)], axis=0),
        slice(0, D))

    my_cols = window(t)
    first = T // quarters
    is_owner = (t >= first) & (t < first + quarters)
    my_j = jnp.clip(t - first, 0, quarters - 1)
    my_quarter = pl.ds(pl.multiple_of(my_j * GW, 128), GW)

    def inside(n):
        return pl.ds(begin(n), Wp)

    span = 8 * CTX
    tiles = BLOCK // 8
    height = tiles * KL * 8 * group
    col = lax.broadcasted_iota(jnp.int32, (height, span), 1)
    row = lax.broadcasted_iota(jnp.int32, (height, span), 0)
    same = (col // CTX) == lax.rem(row, 8)
    spot = lax.rem(col, CTX)
    tail_lane = lax.broadcasted_iota(jnp.int32, (BLOCK, 128), 1)

    def rope(v, cut):
        return (v * cosine[cut] + pltpu.roll(v, half, 1) * sine[cut]).astype(bf16).astype(f32)

    def total_of(ref, index):
        total = jnp.zeros((BLOCK, 1), f32)
        for o in range(quarters):
            tail = index(ref, o).astype(f32)
            total = total + tail[:, 0:1] + tail[:, 64:65]
        return lax.rsqrt(total / D + epsilon)

    def enter(a):
        cut = slice(a * BLOCK, (a + 1) * BLOCK)

        @pl.when(s > 0)
        def _():
            acc = None
            for j in range(quarters):
                wait(ag.at[a, j], ag_rs.at[a, j])
                at = slice(j * GW, (j + 1) * GW)
                p = ag[a, j, :, 0:GW].astype(f32)
                term = matmul((p * pre[:, at]).astype(bf16), at)
                acc = term if acc is None else acc + term
            inv = total_of(ag, lambda ref, o: ref[a, o, :, GW:GW + 128])
            for j in range(quarters):
                at = slice(j * GW, (j + 1) * GW)
                base[a, :, at] = base[a, :, at] + inv * ag[a, j, :, 0:GW].astype(f32)
            x_ref[a] = base[a].astype(bf16)
            proj[cut, :] = proj[cut, :] + inv * acc

        @pl.when((s > 0) & (s < last))
        def _():
            remote(x_ref.at[a], xprev.at[a], xf_ss.at[a], xf_rs.at[a], s + 1, t).start()

        @pl.when(s == last)
        def _():
            for n in range(sper):
                send(x_ref.at[a, :, my_cols], fin_x, fx_ss.at[a, n], fx_rs, a * sper + n, t)

        xf = x_ref[a].astype(f32)
        inv = lax.rsqrt(jnp.mean(xf * xf, axis=1, keepdims=True) + epsilon)
        all_ = proj[cut, :] * inv
        for h in range(H):
            qs[h] = rope(all_[:, h * HD:(h + 1) * HD], cut)
        for h in range(KL):
            c0 = (H + h) * HD
            ks[h] = rope(all_[:, c0:c0 + HD], cut)
            c0 = (H + KL + h) * HD
            vs[h] = all_[:, c0:c0 + HD].astype(bf16).astype(f32)

    def attend(a):
        if a == 0:
            loads[11].wait()
            loads[12].wait()
        units = [(i, h) for i in range(tiles) for h in range(KL)]
        qq = jnp.concatenate([qs[h * group + g, 8 * i:8 * i + 8, :]
                              for i, h in units for g in range(group)], axis=0)
        kk = jnp.concatenate([ks[h, 8 * i:8 * i + 8, :]
                              for i, h in units for g in range(group)], axis=0)
        vv = jnp.concatenate([vs[h, 8 * i:8 * i + 8, :]
                              for i, h in units for g in range(group)], axis=0)
        r0 = a * BLOCK
        limit = jnp.concatenate([lens[r0 + 8 * i:r0 + 8 * i + 8, 0:1]
                                 for i, h in units for g in range(group)], axis=0)
        qb = qq.astype(bf16)
        step = 8 * group
        scores = jnp.concatenate([
            lax.dot_general(qb[n * step:(n + 1) * step],
                            kc_v[r0 + 8 * i:r0 + 8 * i + 8, h].reshape(span, HD),
                            (((1,), (1,)), ((), ())), preferred_element_type=f32)
            for n, (i, h) in enumerate(units)], axis=0) * scale
        own = jnp.sum(qq * kk, axis=1, keepdims=True) * scale
        weight = jnp.where(
            same & (spot < limit),
            jnp.exp(softcap_limit * jnp.tanh(scores / softcap_limit) - softcap_limit), 0.0)
        own_w = jnp.exp(softcap_limit * jnp.tanh(own / softcap_limit) - softcap_limit)
        total = jnp.sum(weight, axis=1, keepdims=True) + own_w
        probs = (weight / total).astype(bf16)
        own_p = (own_w / total).astype(bf16).astype(f32)
        mixed = jnp.concatenate([
            jnp.dot(probs[n * step:(n + 1) * step],
                    vc_v[r0 + 8 * i:r0 + 8 * i + 8, h].reshape(span, HD),
                    preferred_element_type=f32)
            for n, (i, h) in enumerate(units)], axis=0) + own_p * vv
        for n, (i, h) in enumerate(units):
            for g in range(group):
                c0 = (h * group + g) * HD
                heads[8 * i:8 * i + 8, c0:c0 + HD] = mixed[n * step + 8 * g:n * step + 8 * g + 8, :]

    def leave(a):
        if a == 0:
            loads[13].wait()
        hb = heads[...].astype(bf16)
        for j in range(quarters):
            at = slice(j * GW, (j + 1) * GW)
            part[a, j] = jnp.dot(hb, wo_v[:, at], preferred_element_type=f32).astype(bf16)
            send(part.at[a, j], rs.at[a, t], rs_ss.at[a, j], rs_rs.at[a, t], s, first + j)

    def reduce(a):
        @pl.when(is_owner)
        def _():
            summed = jnp.zeros((BLOCK, GW), f32)
            for o in range(T):
                wait(rs.at[a, o], rs_rs.at[a, o])
                summed = summed + rs[a, o].astype(f32)
            squares = jnp.sum(summed * summed, axis=1, keepdims=True)
            high = squares.astype(bf16).astype(f32)
            msg[a, :, 0:GW] = (summed * post[:, my_quarter]).astype(bf16)
            msg[a, :, GW:GW + 128] = jnp.where(tail_lane < 64, high, squares - high).astype(bf16)

        @pl.when(is_owner & (s < last))
        def _():
            for k in range(T):
                dt = lax.rem(t + k, T)
                remote(msg.at[a], ag.at[a, my_j], ag_ss.at[a, k], ag_rs.at[a, my_j],
                       s + 1, dt).start()

        @pl.when(is_owner & (s == last))
        def _():
            for n in range(sper):
                ds = a * sper + n
                for b in range(per):
                    send(msg.at[a, :, inside(b)], fin_p, fp_ss.at[a, n * per + b], fp_rs,
                         ds, my_j * per + b)
                for b in range(T):
                    send(msg.at[a, :, pl.ds(GW, 128)], fin_s.at[my_j], fs_ss.at[a, n * T + b],
                         fs_rs.at[my_j], ds, b)

    for a in range(G):
        enter(a)
        if a > 0:
            reduce(a - 1)
        attend(a)
        leave(a)
    reduce(G - 1)

    wait(fin_x, fx_rs)
    wait(fin_p, fp_rs)
    for o in range(quarters):
        wait(fin_s.at[o], fs_rs.at[o])
    inv = total_of(fin_s, lambda ref, o: ref[o])
    fin_f[...] = fin_x[...].astype(f32) + inv * fin_p[...].astype(f32)
    here = fin_f[pl.ds(pl.multiple_of(lax.rem(s, sper) * rc, rc), rc), :]
    shift = t * W - begin(t)
    piece = here[:, 0:W]
    for b in sorted({(p * W) % 128 for p in range(T)} - {0}):
        piece = jnp.where(shift == b, here[:, b:b + W], piece)
    own_rows = pl.ds(pl.multiple_of(s * rc, rc), rc)
    out_ref[...] = (piece + gates[own_rows, :][:, 0:1] * dself[own_rows, :]).astype(bf16)

    @pl.when(s == 0)
    def _():
        for k in range(1, T):
            wait(resid, xg_ss.at[k])

    for a in range(G):
        for j in range(quarters):
            sent(part.at[a, j], rs_ss.at[a, j], s, first + j)

    @pl.when(s > 0)
    def _():
        for k in range(1, T):
            wait(st.at[t], st_ss.at[k])

    @pl.when(s < last)
    def _():
        for a in range(G):
            wait(x_ref.at[a], xf_ss.at[a])

    @pl.when(is_owner & (s < last))
    def _():
        for a in range(G):
            for k in range(T):
                wait(msg.at[a], ag_ss.at[a, k])

    @pl.when(s == last)
    def _():
        for a in range(G):
            for n in range(sper):
                sent(x_ref.at[a, :, my_cols], fx_ss.at[a, n], a * sper + n, t)

    @pl.when(is_owner & (s == last))
    def _():
        for a in range(G):
            for n in range(sper):
                ds = a * sper + n
                for b in range(per):
                    sent(msg.at[a, :, inside(b)], fp_ss.at[a, n * per + b], ds, my_j * per + b)
                for b in range(T):
                    sent(msg.at[a, :, pl.ds(GW, 128)], fs_ss.at[a, n * T + b], ds, b)


def on_device(
    S, T,
    resid, pre_gain, post_gain, w_query, w_key, w_value, w_out, key_cache, value_cache,
    lengths, concept, steer_layer, strength, directions,
):
    rc, W = resid.shape
    R = lengths.shape[0]
    D = pre_gain.shape[1]
    HD = key_cache.shape[-1]
    H = w_query.shape[2] // HD
    KL = key_cache.shape[2]
    G = R // BLOCK
    Wp = -(-(D // 128) // T) * 128
    chunks = D // 128
    per = next(n for n in range(1, T + 1) if (chunks * n) % T == 0)
    quarters = T // per
    GW = chunks * per // T * 128
    sper = BLOCK // rc
    dma = pltpu.SemaphoreType.DMA
    vm = pltpu.VMEM
    hbm = pl.BlockSpec(memory_space=pltpu.HBM)
    turned = directions.T
    scratch = [
        pltpu.SMEM((R,), jnp.int32), pltpu.SMEM((R,), jnp.int32), pltpu.SMEM((R,), jnp.int32),
        pltpu.SMEM((R,), f32), vm((rc, W), bf16), vm((1, D), f32), vm((1, D), f32),
        vm(w_query.shape[1:], bf16), vm(w_key.shape[1:], bf16), vm(w_value.shape[1:], bf16),
        vm(w_out.shape[1:], bf16), vm(key_cache.shape[1:], bf16), vm(value_cache.shape[1:], bf16),
        vm(turned.shape, bf16),
        vm((S, T, rc, W), bf16), vm((G, BLOCK, D), bf16), vm((G, BLOCK, D), bf16),
        vm((G, BLOCK, D), f32),
        vm((T, R, W), bf16), vm((R, W), f32), vm((R, HD), f32), vm((R, HD), jnp.int32),
        vm((R, (H + 2 * KL) * HD), f32),
        vm((H, BLOCK, HD), f32), vm((KL, BLOCK, HD), f32), vm((KL, BLOCK, HD), f32),
        vm((BLOCK, H * HD), f32),
        vm((G, quarters, BLOCK, GW), bf16), vm((G, T, BLOCK, GW), bf16),
        vm((G, BLOCK, GW + 128), bf16),
        vm((G, quarters, BLOCK, GW + 128), bf16), vm((BLOCK, Wp), bf16), vm((BLOCK, Wp), bf16),
        vm((quarters, BLOCK, 128), bf16), vm((BLOCK, Wp), f32),
        dma((14,)), dma((T,)), dma((S, T)), dma((G,)), dma((G,)), dma((T,)), dma((T,)),
        dma((G, quarters)), dma((G, T)), dma((G, T)), dma((G, quarters)),
        dma((G, sper)), dma, dma((G, sper * per)), dma, dma((G, sper * T)), dma((quarters,)),
    ]
    return pl.pallas_call(
        functools.partial(kernel, S, T),
        out_shape=jax.ShapeDtypeStruct((rc, W), bf16),
        in_specs=[hbm] * 14,
        out_specs=pl.BlockSpec(memory_space=pltpu.VMEM),
        scratch_shapes=scratch,
        compiler_params=pltpu.CompilerParams(
            collective_id=0, has_side_effects=True, vmem_limit_bytes=63 * 1024 * 1024),
    )(lengths, concept, steer_layer, strength, resid, pre_gain, post_gain,
      w_query, w_key, w_value, w_out, key_cache, value_cache, turned)


def solution(mesh):
    placed = (
        P("section", "tensor"),
        P("section", None),
        P("section", None),
        P("section", None, "tensor"),
        P("section", None, "tensor"),
        P("section", None, "tensor"),
        P("section", "tensor", None),
        P("section", None, "tensor", None, None),
        P("section", None, "tensor", None, None),
        P(),
        P(),
        P(),
        P(),
        P(None, "tensor"),
    )
    S, T = mesh.shape["section"], mesh.shape["tensor"]
    return jax.shard_map(
        functools.partial(on_device, S, T), mesh=mesh, in_specs=placed,
        out_specs=P("section", "tensor"), check_vma=False,
    )
```

```python
import functools
import math

import jax
import jax.numpy as jnp
from jax import lax
from jax.experimental import pallas as pl
from jax.experimental.pallas import tpu as pltpu
from jax.sharding import PartitionSpec as P

MESH = pl.DeviceIdType.MESH
epsilon = 1e-06
softcap_limit = 50.0
BLOCK = 16
f32 = jnp.float32
bf16 = jnp.bfloat16


def kernel(
    S, T,
    lengths_h, concept_h, steer_h, strength_h,
    resid_h, pre_h, post_h, wq, wk, wv, wo, kc, vc, dirs,
    out_ref,
    lengths, concept, steer_layer, strength, resid, pre, post,
    wq_v, wk_v, wv_v, wo_v, kc_v, vc_v, dirs_v,
    xg, xprev, x_ref, base, st, dself, gates, lens,
    proj, qs, ks, vs, heads, part, rs, msg, ag, fin_x, fin_p, fin_s, fin_f,
    w_sem, xg_ss, xg_rs, xf_ss, xf_rs, st_ss, st_rs, rs_ss, rs_rs, ag_ss, ag_rs,
    fx_ss, fx_rs, fp_ss, fp_rs, fs_ss, fs_rs,
):
    s = lax.axis_index("section")
    t = lax.axis_index("tensor")
    N = S * T
    G, _, D = x_ref.shape
    R = G * BLOCK
    rc, W = resid.shape
    HD = kc_v.shape[-1]
    CTX = kc_v.shape[2]
    KL = kc_v.shape[1]
    H = qs.shape[0]
    group = H // KL
    chunks = D // 128
    Wp = fin_f.shape[1]
    sper = BLOCK // rc
    per = next(n for n in range(1, T + 1) if (chunks * n) % T == 0)
    quarters = T // per
    GW = chunks * per // T * 128
    last = S - 1
    half = HD // 2
    scale = float(D // (H * T)) ** (-0.5)

    def begin(o):
        return (o * chunks) // T * 128

    def window(o):
        return pl.ds(pl.multiple_of(begin(o), 128), Wp)

    def wait(ref, sem):
        pltpu.make_async_copy(ref, ref, sem).wait()

    def remote(src, dst, ss, rsem, ds, dt):
        return pltpu.make_async_remote_copy(
            src_ref=src, dst_ref=dst, send_sem=ss, recv_sem=rsem,
            device_id=(ds, dt), device_id_type=MESH)

    def send(src, dst, ss, rsem, ds, dt):
        mine = (ds == s) & (dt == t)

        @pl.when(mine)
        def _():
            pltpu.make_async_copy(src, dst, rsem).start()

        @pl.when(jnp.logical_not(mine))
        def _():
            remote(src, dst, ss, rsem, ds, dt).start()

    def sent(src, ss, ds, dt):
        @pl.when(jnp.logical_not((ds == s) & (dt == t)))
        def _():
            wait(src, ss)

    barrier = pltpu.get_barrier_semaphore()
    me = s * T + t

    def greet(n, carry):
        other = lax.rem(me + n, N)
        pl.semaphore_signal(barrier, inc=1, device_id=(other // T, lax.rem(other, T)),
                            device_id_type=MESH)
        return carry

    lax.fori_loop(1, N, greet, 0)

    pairs = [(resid_h, resid), (lengths_h, lengths), (concept_h, concept), (steer_h, steer_layer),
             (strength_h, strength), (pre_h, pre), (post_h, post), (dirs, dirs_v),
             (wq.at[0], wq_v), (wk.at[0], wk_v), (wv.at[0], wv_v), (kc.at[0], kc_v),
             (vc.at[0], vc_v), (wo.at[0], wo_v)]
    loads = [pltpu.make_async_copy(a, b, w_sem.at[i]) for i, (a, b) in enumerate(pairs)]
    for one in loads:
        one.start()
    loads[0].wait()
    pl.semaphore_wait(barrier, N - 1)

    for k in range(T):
        dt = lax.rem(t + k, T)
        send(resid, xg.at[s, t], xg_ss.at[k], xg_rs.at[s, t], 0, dt)

    for n in range(1, 7):
        loads[n].wait()
    rows = lax.broadcasted_iota(jnp.int32, (R, HD), 0)
    zero_i = jnp.zeros((R, HD), jnp.int32)

    def gather(i, carry):
        a, b, c, d = carry
        hit = rows == i
        return (jnp.where(hit, lengths[i], a), jnp.where(hit, concept[i], b),
                jnp.where(hit, steer_layer[i], c), jnp.where(hit, strength[i], d))

    len_v, con_v, lay_v, str_v = lax.fori_loop(
        0, R, gather, (zero_i, zero_i, zero_i, jnp.zeros((R, HD), f32)))
    lens[...] = len_v
    gates[...] = str_v * (lay_v == last).astype(f32)
    lane = lax.broadcasted_iota(jnp.int32, (R, HD), 1)
    frequency = jnp.exp(lax.rem(lane, half).astype(f32) * (-2.0 * math.log(10000.0) / HD))
    angle = len_v.astype(f32) * frequency
    cosine = jnp.cos(angle)
    sine = jnp.sin(angle)
    sine = jnp.where(lane < half, -sine, sine)

    loads[7].wait()
    nc = dirs_v.shape[1]
    one_hot = (con_v[:, 0:1] == lax.broadcasted_iota(jnp.int32, (R, nc), 1)).astype(f32).astype(bf16)
    picked = lax.dot_general(one_hot, dirs_v[...], (((1,), (1,)), ((), ())),
                             preferred_element_type=f32)
    dself[...] = picked

    def matmul(v, part_rows):
        return jnp.concatenate([
            jnp.dot(v, w[part_rows, :], preferred_element_type=f32)
            for w in (wq_v, wk_v, wv_v)], axis=1)

    @pl.when(s == 0)
    def _():
        for a in range(G):
            for n in range(sper):
                owner = a * sper + n
                for b in range(T):
                    wait(xg.at[owner, b], xg_rs.at[owner, b])
                base[a, n * rc:(n + 1) * rc, :] = jnp.concatenate(
                    [xg[owner, b].astype(f32) for b in range(T)], axis=1)
            x_ref[a] = base[a].astype(bf16)
            remote(x_ref.at[a], xprev.at[a], xf_ss.at[a], xf_rs.at[a], s + 1, t).start()

    @pl.when(s > 0)
    def _():
        st[t] = picked.astype(bf16)
        for k in range(T):
            wait(resid, xg_ss.at[k])
        for k in range(1, T):
            dt = lax.rem(t + k, T)
            remote(st.at[t], st.at[t], st_ss.at[k], st_rs.at[t], s, dt).start()
        for k in range(1, T):
            b = lax.rem(t + k, T)
            wait(st.at[b], st_rs.at[b])
        gate = (str_v * (lay_v == s - 1).astype(f32))[:, 0:1]
        full = jnp.concatenate([st[b].astype(f32) for b in range(T)], axis=1)
        for a in range(G):
            cut = slice(a * BLOCK, (a + 1) * BLOCK)
            wait(xprev.at[a], xf_rs.at[a])
            base[a] = xprev[a].astype(f32) + gate[cut] * full[cut]

    for n in (8, 9, 10):
        loads[n].wait()

    def ahead(j, acc):
        at = pl.ds(pl.multiple_of(j * GW, 128), GW)
        known = jnp.concatenate(
            [(base[a, :, at] * pre[:, at]).astype(bf16) for a in range(G)], axis=0)
        return acc + matmul(known, at)

    proj[...] = lax.fori_loop(0, quarters, ahead, jnp.zeros(proj.shape, f32))

    my_cols = window(t)
    first = T // quarters
    is_owner = (t >= first) & (t < first + quarters)
    my_j = jnp.clip(t - first, 0, quarters - 1)
    my_quarter = pl.ds(pl.multiple_of(my_j * GW, 128), GW)

    def inside(n):
        return pl.ds(begin(n), Wp)

    span = 8 * CTX
    tiles = BLOCK // 8
    height = tiles * KL * 8 * group
    col = lax.broadcasted_iota(jnp.int32, (height, span), 1)
    row = lax.broadcasted_iota(jnp.int32, (height, span), 0)
    same = (col // CTX) == lax.rem(row, 8)
    spot = lax.rem(col, CTX)
    tail_lane = lax.broadcasted_iota(jnp.int32, (BLOCK, 128), 1)

    def rope(v, cut):
        return (v * cosine[cut] + pltpu.roll(v, half, 1) * sine[cut]).astype(bf16).astype(f32)

    def total_of(ref, index):
        total = jnp.zeros((BLOCK, 1), f32)
        for o in range(quarters):
            tail = index(ref, o).astype(f32)
            total = total + tail[:, 0:1] + tail[:, 64:65]
        return lax.rsqrt(total / D + epsilon)

    def enter(a):
        cut = slice(a * BLOCK, (a + 1) * BLOCK)

        @pl.when(s > 0)
        def _():
            def arrive(j, acc):
                wait(ag.at[a, j], ag_rs.at[a, j])
                at = pl.ds(pl.multiple_of(j * GW, 128), GW)
                p = ag[a, j, :, 0:GW].astype(f32)
                return acc + matmul((p * pre[:, at]).astype(bf16), at)

            acc = lax.fori_loop(0, quarters, arrive, jnp.zeros((BLOCK, proj.shape[1]), f32))
            inv = total_of(ag, lambda ref, o: ref[a, o, :, GW:GW + 128])
            for j in range(quarters):
                at = slice(j * GW, (j + 1) * GW)
                base[a, :, at] = base[a, :, at] + inv * ag[a, j, :, 0:GW].astype(f32)
            x_ref[a] = base[a].astype(bf16)
            proj[cut, :] = proj[cut, :] + inv * acc

        @pl.when((s > 0) & (s < last))
        def _():
            remote(x_ref.at[a], xprev.at[a], xf_ss.at[a], xf_rs.at[a], s + 1, t).start()

        @pl.when(s == last)
        def _():
            for n in range(sper):
                send(x_ref.at[a, :, my_cols], fin_x, fx_ss.at[a, n], fx_rs, a * sper + n, t)

        xf = x_ref[a].astype(f32)
        inv = lax.rsqrt(jnp.mean(xf * xf, axis=1, keepdims=True) + epsilon)
        all_ = proj[cut, :] * inv
        for h in range(H):
            qs[h] = rope(all_[:, h * HD:(h + 1) * HD], cut)
        for h in range(KL):
            c0 = (H + h) * HD
            ks[h] = rope(all_[:, c0:c0 + HD], cut)
            c0 = (H + KL + h) * HD
            vs[h] = all_[:, c0:c0 + HD].astype(bf16).astype(f32)

    def attend(a):
        if a == 0:
            loads[11].wait()
            loads[12].wait()
        units = [(i, h) for i in range(tiles) for h in range(KL)]
        qq = jnp.concatenate([qs[h * group + g, 8 * i:8 * i + 8, :]
                              for i, h in units for g in range(group)], axis=0)
        kk = jnp.concatenate([ks[h, 8 * i:8 * i + 8, :]
                              for i, h in units for g in range(group)], axis=0)
        vv = jnp.concatenate([vs[h, 8 * i:8 * i + 8, :]
                              for i, h in units for g in range(group)], axis=0)
        r0 = a * BLOCK
        limit = jnp.concatenate([lens[r0 + 8 * i:r0 + 8 * i + 8, 0:1]
                                 for i, h in units for g in range(group)], axis=0)
        qb = qq.astype(bf16)
        step = 8 * group
        scores = jnp.concatenate([
            lax.dot_general(qb[n * step:(n + 1) * step],
                            kc_v[r0 + 8 * i:r0 + 8 * i + 8, h].reshape(span, HD),
                            (((1,), (1,)), ((), ())), preferred_element_type=f32)
            for n, (i, h) in enumerate(units)], axis=0) * scale
        own = jnp.sum(qq * kk, axis=1, keepdims=True) * scale
        weight = jnp.where(
            same & (spot < limit),
            jnp.exp(softcap_limit * jnp.tanh(scores / softcap_limit) - softcap_limit), 0.0)
        own_w = jnp.exp(softcap_limit * jnp.tanh(own / softcap_limit) - softcap_limit)
        total = jnp.sum(weight, axis=1, keepdims=True) + own_w
        probs = (weight / total).astype(bf16)
        own_p = (own_w / total).astype(bf16).astype(f32)
        mixed = jnp.concatenate([
            jnp.dot(probs[n * step:(n + 1) * step],
                    vc_v[r0 + 8 * i:r0 + 8 * i + 8, h].reshape(span, HD),
                    preferred_element_type=f32)
            for n, (i, h) in enumerate(units)], axis=0) + own_p * vv
        for n, (i, h) in enumerate(units):
            for g in range(group):
                c0 = (h * group + g) * HD
                heads[8 * i:8 * i + 8, c0:c0 + HD] = mixed[n * step + 8 * g:n * step + 8 * g + 8, :]

    def leave(a):
        if a == 0:
            loads[13].wait()
        hb = heads[...].astype(bf16)

        def quarter(j, carry):
            at = pl.ds(pl.multiple_of(j * GW, 128), GW)
            part[a, j] = jnp.dot(hb, wo_v[:, at], preferred_element_type=f32).astype(bf16)
            send(part.at[a, j], rs.at[a, t], rs_ss.at[a, j], rs_rs.at[a, t], s, first + j)
            return carry

        lax.fori_loop(0, quarters, quarter, 0)

    def reduce(a):
        @pl.when(is_owner)
        def _():
            summed = jnp.zeros((BLOCK, GW), f32)
            for o in range(T):
                wait(rs.at[a, o], rs_rs.at[a, o])
                summed = summed + rs[a, o].astype(f32)
            squares = jnp.sum(summed * summed, axis=1, keepdims=True)
            high = squares.astype(bf16).astype(f32)
            msg[a, :, 0:GW] = (summed * post[:, my_quarter]).astype(bf16)
            msg[a, :, GW:GW + 128] = jnp.where(tail_lane < 64, high, squares - high).astype(bf16)

        @pl.when(is_owner & (s < last))
        def _():
            for k in range(T):
                dt = lax.rem(t + k, T)
                remote(msg.at[a], ag.at[a, my_j], ag_ss.at[a, k], ag_rs.at[a, my_j],
                       s + 1, dt).start()

        @pl.when(is_owner & (s == last))
        def _():
            for n in range(sper):
                ds = a * sper + n
                for b in range(per):
                    send(msg.at[a, :, inside(b)], fin_p, fp_ss.at[a, n * per + b], fp_rs,
                         ds, my_j * per + b)

                def tell(b, carry):
                    send(msg.at[a, :, pl.ds(GW, 128)], fin_s.at[my_j], fs_ss.at[a, n * T + b],
                         fs_rs.at[my_j], ds, b)
                    return carry

                lax.fori_loop(0, T, tell, 0)

    for a in range(G):
        enter(a)
        if a > 0:
            reduce(a - 1)
        attend(a)
        leave(a)
    reduce(G - 1)

    wait(fin_x, fx_rs)
    wait(fin_p, fp_rs)
    for o in range(quarters):
        wait(fin_s.at[o], fs_rs.at[o])
    inv = total_of(fin_s, lambda ref, o: ref[o])
    fin_f[...] = fin_x[...].astype(f32) + inv * fin_p[...].astype(f32)
    here = fin_f[pl.ds(pl.multiple_of(lax.rem(s, sper) * rc, rc), rc), :]
    shift = t * W - begin(t)
    piece = here[:, 0:W]
    for b in sorted({(p * W) % 128 for p in range(T)} - {0}):
        piece = jnp.where(shift == b, here[:, b:b + W], piece)
    own_rows = pl.ds(pl.multiple_of(s * rc, rc), rc)
    out_ref[...] = (piece + gates[own_rows, :][:, 0:1] * dself[own_rows, :]).astype(bf16)

    @pl.when(s == 0)
    def _():
        for k in range(1, T):
            wait(resid, xg_ss.at[k])

    for a in range(G):
        for j in range(quarters):
            sent(part.at[a, j], rs_ss.at[a, j], s, first + j)

    @pl.when(s > 0)
    def _():
        for k in range(1, T):
            wait(st.at[t], st_ss.at[k])

    @pl.when(s < last)
    def _():
        for a in range(G):
            wait(x_ref.at[a], xf_ss.at[a])

    @pl.when(is_owner & (s < last))
    def _():
        for a in range(G):
            for k in range(T):
                wait(msg.at[a], ag_ss.at[a, k])

    @pl.when(s == last)
    def _():
        for a in range(G):
            for n in range(sper):
                sent(x_ref.at[a, :, my_cols], fx_ss.at[a, n], a * sper + n, t)

    @pl.when(is_owner & (s == last))
    def _():
        for a in range(G):
            for n in range(sper):
                ds = a * sper + n
                for b in range(per):
                    sent(msg.at[a, :, inside(b)], fp_ss.at[a, n * per + b], ds, my_j * per + b)
                for b in range(T):
                    sent(msg.at[a, :, pl.ds(GW, 128)], fs_ss.at[a, n * T + b], ds, b)


def on_device(
    S, T,
    resid, pre_gain, post_gain, w_query, w_key, w_value, w_out, key_cache, value_cache,
    lengths, concept, steer_layer, strength, directions,
):
    rc, W = resid.shape
    R = lengths.shape[0]
    D = pre_gain.shape[1]
    HD = key_cache.shape[-1]
    H = w_query.shape[2] // HD
    KL = key_cache.shape[2]
    G = R // BLOCK
    Wp = -(-(D // 128) // T) * 128
    chunks = D // 128
    per = next(n for n in range(1, T + 1) if (chunks * n) % T == 0)
    quarters = T // per
    GW = chunks * per // T * 128
    sper = BLOCK // rc
    dma = pltpu.SemaphoreType.DMA
    vm = pltpu.VMEM
    hbm = pl.BlockSpec(memory_space=pltpu.HBM)
    turned = directions.T
    scratch = [
        pltpu.SMEM((R,), jnp.int32), pltpu.SMEM((R,), jnp.int32), pltpu.SMEM((R,), jnp.int32),
        pltpu.SMEM((R,), f32), vm((rc, W), bf16), vm((1, D), f32), vm((1, D), f32),
        vm(w_query.shape[1:], bf16), vm(w_key.shape[1:], bf16), vm(w_value.shape[1:], bf16),
        vm(w_out.shape[1:], bf16), vm(key_cache.shape[1:], bf16), vm(value_cache.shape[1:], bf16),
        vm(turned.shape, bf16),
        vm((S, T, rc, W), bf16), vm((G, BLOCK, D), bf16), vm((G, BLOCK, D), bf16),
        vm((G, BLOCK, D), f32),
        vm((T, R, W), bf16), vm((R, W), f32), vm((R, HD), f32), vm((R, HD), jnp.int32),
        vm((R, (H + 2 * KL) * HD), f32),
        vm((H, BLOCK, HD), f32), vm((KL, BLOCK, HD), f32), vm((KL, BLOCK, HD), f32),
        vm((BLOCK, H * HD), f32),
        vm((G, quarters, BLOCK, GW), bf16), vm((G, T, BLOCK, GW), bf16),
        vm((G, BLOCK, GW + 128), bf16),
        vm((G, quarters, BLOCK, GW + 128), bf16), vm((BLOCK, Wp), bf16), vm((BLOCK, Wp), bf16),
        vm((quarters, BLOCK, 128), bf16), vm((BLOCK, Wp), f32),
        dma((14,)), dma((T,)), dma((S, T)), dma((G,)), dma((G,)), dma((T,)), dma((T,)),
        dma((G, quarters)), dma((G, T)), dma((G, T)), dma((G, quarters)),
        dma((G, sper)), dma, dma((G, sper * per)), dma, dma((G, sper * T)), dma((quarters,)),
    ]
    return pl.pallas_call(
        functools.partial(kernel, S, T),
        out_shape=jax.ShapeDtypeStruct((rc, W), bf16),
        in_specs=[hbm] * 14,
        out_specs=pl.BlockSpec(memory_space=pltpu.VMEM),
        scratch_shapes=scratch,
        compiler_params=pltpu.CompilerParams(
            collective_id=0, has_side_effects=True, vmem_limit_bytes=63 * 1024 * 1024),
    )(lengths, concept, steer_layer, strength, resid, pre_gain, post_gain,
      w_query, w_key, w_value, w_out, key_cache, value_cache, turned)


def solution(mesh):
    placed = (
        P("section", "tensor"),
        P("section", None),
        P("section", None),
        P("section", None, "tensor"),
        P("section", None, "tensor"),
        P("section", None, "tensor"),
        P("section", "tensor", None),
        P("section", None, "tensor", None, None),
        P("section", None, "tensor", None, None),
        P(),
        P(),
        P(),
        P(),
        P(None, "tensor"),
    )
    S, T = mesh.shape["section"], mesh.shape["tensor"]
    return jax.shard_map(
        functools.partial(on_device, S, T), mesh=mesh, in_specs=placed,
        out_specs=P("section", "tensor"), check_vma=False,
    )
```

```python
import functools
import math

import jax
import jax.numpy as jnp
from jax import lax
from jax.experimental import pallas as pl
from jax.experimental.pallas import tpu as pltpu
from jax.sharding import PartitionSpec as P

MESH = pl.DeviceIdType.MESH
epsilon = 1e-06
softcap_limit = 50.0
BLOCK = 16
f32 = jnp.float32
bf16 = jnp.bfloat16


def kernel(
    S, T,
    lengths_h, concept_h, steer_h, strength_h,
    resid_h, pre_h, post_h, wq, wk, wv, wo, kc, vc, dirs,
    out_ref,
    lengths, concept, steer_layer, strength, resid, pre, post,
    wq_v, wk_v, wv_v, wo_v, kc_v, vc_v, dirs_v,
    xg, xprev, x_ref, base, st, dself, gates, lens,
    proj, qs, ks, vs, heads, part, rs, msg, ag, fin_x, fin_p, fin_s, fin_f,
    w_sem, xg_ss, xg_rs, xf_ss, xf_rs, st_ss, st_rs, rs_ss, rs_rs, ag_ss, ag_rs,
    fx_ss, fx_rs, fp_ss, fp_rs, fs_ss, fs_rs,
):
    s = lax.axis_index("section")
    t = lax.axis_index("tensor")
    N = S * T
    G, _, D = x_ref.shape
    R = G * BLOCK
    rc, W = resid.shape
    HD = kc_v.shape[-1]
    CTX = kc_v.shape[2]
    KL = kc_v.shape[1]
    H = qs.shape[0]
    group = H // KL
    chunks = D // 128
    Wp = fin_f.shape[1]
    sper = BLOCK // rc
    per = next(n for n in range(1, T + 1) if (chunks * n) % T == 0)
    quarters = T // per
    GW = chunks * per // T * 128
    last = S - 1
    half = HD // 2
    scale = float(D // (H * T)) ** (-0.5)

    def begin(o):
        return (o * chunks) // T * 128

    def window(o):
        return pl.ds(pl.multiple_of(begin(o), 128), Wp)

    def wait(ref, sem):
        pltpu.make_async_copy(ref, ref, sem).wait()

    def remote(src, dst, ss, rsem, ds, dt):
        return pltpu.make_async_remote_copy(
            src_ref=src, dst_ref=dst, send_sem=ss, recv_sem=rsem,
            device_id=(ds, dt), device_id_type=MESH)

    def send(src, dst, ss, rsem, ds, dt):
        mine = (ds == s) & (dt == t)

        @pl.when(mine)
        def _():
            pltpu.make_async_copy(src, dst, rsem).start()

        @pl.when(jnp.logical_not(mine))
        def _():
            remote(src, dst, ss, rsem, ds, dt).start()

    def sent(src, ss, ds, dt):
        @pl.when(jnp.logical_not((ds == s) & (dt == t)))
        def _():
            wait(src, ss)

    barrier = pltpu.get_barrier_semaphore()
    me = s * T + t

    def greet(n, carry):
        other = lax.rem(me + n, N)
        pl.semaphore_signal(barrier, inc=1, device_id=(other // T, lax.rem(other, T)),
                            device_id_type=MESH)
        return carry

    lax.fori_loop(1, N, greet, 0)

    pairs = [(resid_h, resid), (lengths_h, lengths), (concept_h, concept), (steer_h, steer_layer),
             (strength_h, strength), (pre_h, pre), (post_h, post), (dirs, dirs_v),
             (wq.at[0], wq_v), (wk.at[0], wk_v), (wv.at[0], wv_v), (kc.at[0], kc_v),
             (vc.at[0], vc_v), (wo.at[0], wo_v)]
    loads = [pltpu.make_async_copy(a, b, w_sem.at[i]) for i, (a, b) in enumerate(pairs)]
    for one in loads:
        one.start()
    loads[0].wait()
    pl.semaphore_wait(barrier, N - 1)

    for k in range(T):
        dt = lax.rem(t + k, T)
        send(resid, xg.at[s, t], xg_ss.at[k], xg_rs.at[s, t], 0, dt)

    for n in range(1, 7):
        loads[n].wait()
    rows = lax.broadcasted_iota(jnp.int32, (R, HD), 0)
    zero_i = jnp.zeros((R, HD), jnp.int32)

    def gather(i, carry):
        a, b, c, d = carry
        hit = rows == i
        return (jnp.where(hit, lengths[i], a), jnp.where(hit, concept[i], b),
                jnp.where(hit, steer_layer[i], c), jnp.where(hit, strength[i], d))

    len_v, con_v, lay_v, str_v = lax.fori_loop(
        0, R, gather, (zero_i, zero_i, zero_i, jnp.zeros((R, HD), f32)))
    lens[...] = len_v
    gates[...] = str_v * (lay_v == last).astype(f32)
    lane = lax.broadcasted_iota(jnp.int32, (R, HD), 1)
    frequency = jnp.exp(lax.rem(lane, half).astype(f32) * (-2.0 * math.log(10000.0) / HD))
    angle = len_v.astype(f32) * frequency
    cosine = jnp.cos(angle)
    sine = jnp.sin(angle)
    sine = jnp.where(lane < half, -sine, sine)

    loads[7].wait()
    nc = dirs_v.shape[1]
    one_hot = (con_v[:, 0:1] == lax.broadcasted_iota(jnp.int32, (R, nc), 1)).astype(f32).astype(bf16)
    picked = lax.dot_general(one_hot, dirs_v[...], (((1,), (1,)), ((), ())),
                             preferred_element_type=f32)
    dself[...] = picked

    def matmul(v, part_rows):
        return jnp.concatenate([
            jnp.dot(v, w[part_rows, :], preferred_element_type=f32)
            for w in (wq_v, wk_v, wv_v)], axis=1)

    @pl.when(s == 0)
    def _():
        for a in range(G):
            for n in range(sper):
                owner = a * sper + n
                for b in range(T):
                    wait(xg.at[owner, b], xg_rs.at[owner, b])
                base[a, n * rc:(n + 1) * rc, :] = jnp.concatenate(
                    [xg[owner, b].astype(f32) for b in range(T)], axis=1)
            x_ref[a] = base[a].astype(bf16)
            remote(x_ref.at[a], xprev.at[a], xf_ss.at[a], xf_rs.at[a], s + 1, t).start()

    @pl.when(s > 0)
    def _():
        st[t] = picked.astype(bf16)
        for k in range(T):
            wait(resid, xg_ss.at[k])
        for k in range(1, T):
            dt = lax.rem(t + k, T)
            remote(st.at[t], st.at[t], st_ss.at[k], st_rs.at[t], s, dt).start()
        for k in range(1, T):
            b = lax.rem(t + k, T)
            wait(st.at[b], st_rs.at[b])
        gate = (str_v * (lay_v == s - 1).astype(f32))[:, 0:1]
        full = jnp.concatenate([st[b].astype(f32) for b in range(T)], axis=1)
        for a in range(G):
            cut = slice(a * BLOCK, (a + 1) * BLOCK)
            wait(xprev.at[a], xf_rs.at[a])
            base[a] = xprev[a].astype(f32) + gate[cut] * full[cut]

    for n in (8, 9, 10):
        loads[n].wait()
    proj[...] = matmul(
        jnp.concatenate([(base[a] * pre[...]).astype(bf16) for a in range(G)], axis=0),
        slice(0, D))

    my_cols = window(t)
    first = T // quarters
    is_owner = (t >= first) & (t < first + quarters)
    my_j = jnp.clip(t - first, 0, quarters - 1)
    my_quarter = pl.ds(pl.multiple_of(my_j * GW, 128), GW)

    def inside(n):
        return pl.ds(begin(n), Wp)

    span = 8 * CTX
    tiles = BLOCK // 8
    height = tiles * KL * 8 * group
    col = lax.broadcasted_iota(jnp.int32, (height, span), 1)
    row = lax.broadcasted_iota(jnp.int32, (height, span), 0)
    same = (col // CTX) == lax.rem(row, 8)
    spot = lax.rem(col, CTX)
    tail_lane = lax.broadcasted_iota(jnp.int32, (BLOCK, 128), 1)

    def rope(v, cut):
        return (v * cosine[cut] + pltpu.roll(v, half, 1) * sine[cut]).astype(bf16).astype(f32)

    def total_of(ref, index):
        total = jnp.zeros((BLOCK, 1), f32)
        for o in range(quarters):
            tail = index(ref, o).astype(f32)
            total = total + tail[:, 0:1] + tail[:, 64:65]
        return lax.rsqrt(total / D + epsilon)

    def enter(a):
        cut = slice(a * BLOCK, (a + 1) * BLOCK)

        @pl.when(s > 0)
        def _():
            acc = None
            for j in range(quarters):
                wait(ag.at[a, j], ag_rs.at[a, j])
                at = slice(j * GW, (j + 1) * GW)
                p = ag[a, j, :, 0:GW].astype(f32)
                term = matmul((p * pre[:, at]).astype(bf16), at)
                acc = term if acc is None else acc + term
            inv = total_of(ag, lambda ref, o: ref[a, o, :, GW:GW + 128])
            for j in range(quarters):
                at = slice(j * GW, (j + 1) * GW)
                base[a, :, at] = base[a, :, at] + inv * ag[a, j, :, 0:GW].astype(f32)
            x_ref[a] = base[a].astype(bf16)
            proj[cut, :] = proj[cut, :] + inv * acc

        @pl.when((s > 0) & (s < last))
        def _():
            remote(x_ref.at[a], xprev.at[a], xf_ss.at[a], xf_rs.at[a], s + 1, t).start()

        @pl.when(s == last)
        def _():
            for n in range(sper):
                send(x_ref.at[a, :, my_cols], fin_x, fx_ss.at[a, n], fx_rs, a * sper + n, t)

        xf = x_ref[a].astype(f32)
        inv = lax.rsqrt(jnp.mean(xf * xf, axis=1, keepdims=True) + epsilon)
        all_ = proj[cut, :] * inv
        for h in range(H):
            qs[h] = rope(all_[:, h * HD:(h + 1) * HD], cut)
        for h in range(KL):
            c0 = (H + h) * HD
            ks[h] = rope(all_[:, c0:c0 + HD], cut)
            c0 = (H + KL + h) * HD
            vs[h] = all_[:, c0:c0 + HD].astype(bf16).astype(f32)

    def attend(a):
        if a == 0:
            loads[11].wait()
            loads[12].wait()
        units = [(i, h) for i in range(tiles) for h in range(KL)]
        qq = jnp.concatenate([qs[h * group + g, 8 * i:8 * i + 8, :]
                              for i, h in units for g in range(group)], axis=0)
        kk = jnp.concatenate([ks[h, 8 * i:8 * i + 8, :]
                              for i, h in units for g in range(group)], axis=0)
        vv = jnp.concatenate([vs[h, 8 * i:8 * i + 8, :]
                              for i, h in units for g in range(group)], axis=0)
        r0 = a * BLOCK
        limit = jnp.concatenate([lens[r0 + 8 * i:r0 + 8 * i + 8, 0:1]
                                 for i, h in units for g in range(group)], axis=0)
        qb = qq.astype(bf16)
        step = 8 * group
        scores = jnp.concatenate([
            lax.dot_general(qb[n * step:(n + 1) * step],
                            kc_v[r0 + 8 * i:r0 + 8 * i + 8, h].reshape(span, HD),
                            (((1,), (1,)), ((), ())), preferred_element_type=f32)
            for n, (i, h) in enumerate(units)], axis=0) * scale
        own = jnp.sum(qq * kk, axis=1, keepdims=True) * scale
        weight = jnp.where(
            same & (spot < limit),
            jnp.exp(softcap_limit * jnp.tanh(scores / softcap_limit) - softcap_limit), 0.0)
        own_w = jnp.exp(softcap_limit * jnp.tanh(own / softcap_limit) - softcap_limit)
        total = jnp.sum(weight, axis=1, keepdims=True) + own_w
        probs = (weight / total).astype(bf16)
        own_p = (own_w / total).astype(bf16).astype(f32)
        mixed = jnp.concatenate([
            jnp.dot(probs[n * step:(n + 1) * step],
                    vc_v[r0 + 8 * i:r0 + 8 * i + 8, h].reshape(span, HD),
                    preferred_element_type=f32)
            for n, (i, h) in enumerate(units)], axis=0) + own_p * vv
        for n, (i, h) in enumerate(units):
            for g in range(group):
                c0 = (h * group + g) * HD
                heads[8 * i:8 * i + 8, c0:c0 + HD] = mixed[n * step + 8 * g:n * step + 8 * g + 8, :]

    def leave(a):
        if a == 0:
            loads[13].wait()
        hb = heads[...].astype(bf16)
        for i in range(quarters):
            j = lax.rem(t + i, quarters)
            at = pl.ds(pl.multiple_of(j * GW, 128), GW)
            part[a, j] = jnp.dot(hb, wo_v[:, at], preferred_element_type=f32).astype(bf16)
            send(part.at[a, j], rs.at[a, t], rs_ss.at[a, j], rs_rs.at[a, t], s, first + j)

    def reduce(a):
        @pl.when(is_owner)
        def _():
            summed = jnp.zeros((BLOCK, GW), f32)
            for o in range(T):
                wait(rs.at[a, o], rs_rs.at[a, o])
                summed = summed + rs[a, o].astype(f32)
            squares = jnp.sum(summed * summed, axis=1, keepdims=True)
            high = squares.astype(bf16).astype(f32)
            msg[a, :, 0:GW] = (summed * post[:, my_quarter]).astype(bf16)
            msg[a, :, GW:GW + 128] = jnp.where(tail_lane < 64, high, squares - high).astype(bf16)

        @pl.when(is_owner & (s < last))
        def _():
            for k in range(T):
                dt = lax.rem(t + k, T)
                remote(msg.at[a], ag.at[a, my_j], ag_ss.at[a, k], ag_rs.at[a, my_j],
                       s + 1, dt).start()

        @pl.when(is_owner & (s == last))
        def _():
            for n in range(sper):
                ds = a * sper + n
                for b in range(per):
                    send(msg.at[a, :, inside(b)], fin_p, fp_ss.at[a, n * per + b], fp_rs,
                         ds, my_j * per + b)
                for b in range(T):
                    send(msg.at[a, :, pl.ds(GW, 128)], fin_s.at[my_j], fs_ss.at[a, n * T + b],
                         fs_rs.at[my_j], ds, b)

    for a in range(G):
        enter(a)
        if a > 0:
            reduce(a - 1)
        attend(a)
        leave(a)
    reduce(G - 1)

    wait(fin_x, fx_rs)
    wait(fin_p, fp_rs)
    for o in range(quarters):
        wait(fin_s.at[o], fs_rs.at[o])
    inv = total_of(fin_s, lambda ref, o: ref[o])
    fin_f[...] = fin_x[...].astype(f32) + inv * fin_p[...].astype(f32)
    here = fin_f[pl.ds(pl.multiple_of(lax.rem(s, sper) * rc, rc), rc), :]
    shift = t * W - begin(t)
    piece = here[:, 0:W]
    for b in sorted({(p * W) % 128 for p in range(T)} - {0}):
        piece = jnp.where(shift == b, here[:, b:b + W], piece)
    own_rows = pl.ds(pl.multiple_of(s * rc, rc), rc)
    out_ref[...] = (piece + gates[own_rows, :][:, 0:1] * dself[own_rows, :]).astype(bf16)

    @pl.when(s == 0)
    def _():
        for k in range(1, T):
            wait(resid, xg_ss.at[k])

    for a in range(G):
        for j in range(quarters):
            sent(part.at[a, j], rs_ss.at[a, j], s, first + j)

    @pl.when(s > 0)
    def _():
        for k in range(1, T):
            wait(st.at[t], st_ss.at[k])

    @pl.when(s < last)
    def _():
        for a in range(G):
            wait(x_ref.at[a], xf_ss.at[a])

    @pl.when(is_owner & (s < last))
    def _():
        for a in range(G):
            for k in range(T):
                wait(msg.at[a], ag_ss.at[a, k])

    @pl.when(s == last)
    def _():
        for a in range(G):
            for n in range(sper):
                sent(x_ref.at[a, :, my_cols], fx_ss.at[a, n], a * sper + n, t)

    @pl.when(is_owner & (s == last))
    def _():
        for a in range(G):
            for n in range(sper):
                ds = a * sper + n
                for b in range(per):
                    sent(msg.at[a, :, inside(b)], fp_ss.at[a, n * per + b], ds, my_j * per + b)
                for b in range(T):
                    sent(msg.at[a, :, pl.ds(GW, 128)], fs_ss.at[a, n * T + b], ds, b)


def on_device(
    S, T,
    resid, pre_gain, post_gain, w_query, w_key, w_value, w_out, key_cache, value_cache,
    lengths, concept, steer_layer, strength, directions,
):
    rc, W = resid.shape
    R = lengths.shape[0]
    D = pre_gain.shape[1]
    HD = key_cache.shape[-1]
    H = w_query.shape[2] // HD
    KL = key_cache.shape[2]
    G = R // BLOCK
    Wp = -(-(D // 128) // T) * 128
    chunks = D // 128
    per = next(n for n in range(1, T + 1) if (chunks * n) % T == 0)
    quarters = T // per
    GW = chunks * per // T * 128
    sper = BLOCK // rc
    dma = pltpu.SemaphoreType.DMA
    vm = pltpu.VMEM
    hbm = pl.BlockSpec(memory_space=pltpu.HBM)
    turned = directions.T
    scratch = [
        pltpu.SMEM((R,), jnp.int32), pltpu.SMEM((R,), jnp.int32), pltpu.SMEM((R,), jnp.int32),
        pltpu.SMEM((R,), f32), vm((rc, W), bf16), vm((1, D), f32), vm((1, D), f32),
        vm(w_query.shape[1:], bf16), vm(w_key.shape[1:], bf16), vm(w_value.shape[1:], bf16),
        vm(w_out.shape[1:], bf16), vm(key_cache.shape[1:], bf16), vm(value_cache.shape[1:], bf16),
        vm(turned.shape, bf16),
        vm((S, T, rc, W), bf16), vm((G, BLOCK, D), bf16), vm((G, BLOCK, D), bf16),
        vm((G, BLOCK, D), f32),
        vm((T, R, W), bf16), vm((R, W), f32), vm((R, HD), f32), vm((R, HD), jnp.int32),
        vm((R, (H + 2 * KL) * HD), f32),
        vm((H, BLOCK, HD), f32), vm((KL, BLOCK, HD), f32), vm((KL, BLOCK, HD), f32),
        vm((BLOCK, H * HD), f32),
        vm((G, quarters, BLOCK, GW), bf16), vm((G, T, BLOCK, GW), bf16),
        vm((G, BLOCK, GW + 128), bf16),
        vm((G, quarters, BLOCK, GW + 128), bf16), vm((BLOCK, Wp), bf16), vm((BLOCK, Wp), bf16),
        vm((quarters, BLOCK, 128), bf16), vm((BLOCK, Wp), f32),
        dma((14,)), dma((T,)), dma((S, T)), dma((G,)), dma((G,)), dma((T,)), dma((T,)),
        dma((G, quarters)), dma((G, T)), dma((G, T)), dma((G, quarters)),
        dma((G, sper)), dma, dma((G, sper * per)), dma, dma((G, sper * T)), dma((quarters,)),
    ]
    return pl.pallas_call(
        functools.partial(kernel, S, T),
        out_shape=jax.ShapeDtypeStruct((rc, W), bf16),
        in_specs=[hbm] * 14,
        out_specs=pl.BlockSpec(memory_space=pltpu.VMEM),
        scratch_shapes=scratch,
        compiler_params=pltpu.CompilerParams(
            collective_id=0, has_side_effects=True, vmem_limit_bytes=63 * 1024 * 1024),
    )(lengths, concept, steer_layer, strength, resid, pre_gain, post_gain,
      w_query, w_key, w_value, w_out, key_cache, value_cache, turned)


def solution(mesh):
    placed = (
        P("section", "tensor"),
        P("section", None),
        P("section", None),
        P("section", None, "tensor"),
        P("section", None, "tensor"),
        P("section", None, "tensor"),
        P("section", "tensor", None),
        P("section", None, "tensor", None, None),
        P("section", None, "tensor", None, None),
        P(),
        P(),
        P(),
        P(),
        P(None, "tensor"),
    )
    S, T = mesh.shape["section"], mesh.shape["tensor"]
    return jax.shard_map(
        functools.partial(on_device, S, T), mesh=mesh, in_specs=placed,
        out_specs=P("section", "tensor"), check_vma=False,
    )
```
